32 devices in a mesh: groups: 2 (over y), rep: 4 (over z), fsdp: 2 (over x), tp: 2 (over core).
Axes of the slice: x: 2, y: 2, z: 4, core: 2. Of those that a mesh axis runs over, the one named last changes fastest.
Arguments:
- tokens: bfloat16 [10240, 5120], P(('groups', 'rep', 'fsdp'), 'tp'), parts along dimension 0, may hold values from -6 to 6
- norm_gain: bfloat16 [5120], replicated, may hold values from 0.099609375 to 1.8984375
- key_weight: bfloat16 [5120, 512], P('fsdp', 'tp'), may hold values from -0.078125 to 0.078125
- value_weight: bfloat16 [5120, 512], P('fsdp', 'tp'), may hold values from -0.078125 to 0.078125
- key_bias: bfloat16 [512], P('tp'), may hold values from -3 to 3
- value_bias: bfloat16 [512], P('tp'), may hold values from -3 to 3
- block_counts: int32 [16], P('groups'), parts along dimension 0, may hold values from 1 to 5, as said below
- positions: int32 [10240], P(('groups', 'rep', 'fsdp')), parts along dimension 0, may hold values from 0 to 32767
- dest_slots: int32 [10240], P(('groups', 'rep', 'fsdp')), parts along dimension 0, may hold values from -1 to 2047, as said below
Outputs:
- cache_keys: bfloat16 [4096, 512], P(('groups', 'rep', 'fsdp'), 'tp'), parts along dimension 0
- cache_values: bfloat16 [4096, 512], P(('groups', 'rep', 'fsdp'), 'tp'), parts along dimension 0
The draws below stay inside these ranges and needn't reach their ends.
There are 2 independent parts, one for each index of `groups`. The reference program is written for one: setup_inputs(seed, part) draws one part's arguments, and reference() takes and returns one part's arrays. A program takes and returns all parts, laid end to end along the dimension named above; an argument that names none is the same for every part. Nothing has to cross between parts.
Inputs may be any that keep to these rules, and one draw needn't show every extreme that they name: `block_counts`: valid rows come first on each device. One device has 5 blocks, three have 1, all others 2. `dest_slots`: valid rows name distinct cache rows and every cache row is named once; cache rows k * 256 to (k + 1) * 256 - 1 belong to device k of the group; the rows of one device name at most 96 cache rows of one owner, and some device reaches it; padding rows hold -1.
All inputs are finite; a program needn't handle non-finite values.
Results may differ from the reference program's by a relative error of at most 0.0046.
Values may be sent and summed in bfloat16 or wider, within the bound.
No kernel may reach another device: no remote copies, remote signals or barrier semaphores. Data moves between devices by JAX's collectives and lax.ppermute only.
A program may use at most 64 MiB of HBM per device.

```python
import jax
import jax.numpy as jnp
from jax import lax

D = 5120
HEAD_DIM = 128
BLOCK = 128
HOT_BLOCKS = 5
OWN_BLOCKS = 2
KVW = 512
DEVS = 8
TOK_DEV = 640
OWN_DEV = 256
ROWS = 5120
OUT_ROWS = 2048


def layout(key):
    devices = DEVS
    unit_rows = BLOCK // DEVS
    device_rank = jnp.argsort(jax.random.permutation(jax.random.fold_in(key, 101), devices))
    blocks = jnp.where(device_rank == 0, HOT_BLOCKS, jnp.where(device_rank <= devices - 4, OWN_BLOCKS, 1)).astype(jnp.int32)
    sign_rows = jnp.where(jnp.argsort(jax.random.permutation(jax.random.fold_in(key, 102), devices)) < devices // 2, 1, -1).astype(jnp.int32)
    sign_cols = jnp.where(jnp.argsort(jax.random.permutation(jax.random.fold_in(key, 103), devices)) < devices // 2, 1, -1).astype(jnp.int32)
    row_share = unit_rows * (blocks[:, None] + sign_rows[:, None] * sign_cols[None, :])
    share_bound = jnp.cumsum(row_share, axis=1)
    local_index = jnp.arange(TOK_DEV, dtype=jnp.int32)
    owner_index = jnp.sum((share_bound[:, None, :] <= local_index[None, :, None]).astype(jnp.int32), axis=2)
    is_live = local_index[None, :] < BLOCK * blocks[:, None]
    jitter_bits = jax.random.randint(jax.random.fold_in(key, 104), (devices, TOK_DEV), 0, 1 << 20)
    sort_score = jnp.where(is_live, jitter_bits * TOK_DEV + local_index[None, :], (1 << 30) + local_index[None, :])
    shuffled = jnp.argsort(sort_score, axis=1, stable=True)
    owner_index = jnp.clip(jnp.take_along_axis(owner_index, shuffled, axis=1), 0, devices - 1)
    offset_rows = jnp.cumsum(row_share, axis=0) - row_share
    onehot = ((owner_index[:, :, None] == jnp.arange(devices, dtype=jnp.int32)[None, None, :]) & is_live[:, :, None]).astype(jnp.int32)
    rank_in_slot = jnp.sum((jnp.cumsum(onehot, axis=1) - 1) * onehot, axis=2)
    begin_rows = jnp.take_along_axis(offset_rows, owner_index, axis=1)
    dest = jnp.where(is_live, owner_index * OWN_DEV + begin_rows + rank_in_slot, -1)
    return (blocks, dest.reshape(-1).astype(jnp.int32))


def draw_block_counts(key, part):
    blocks, dest = layout(key)
    return blocks


def draw_dest_slots(key, part):
    blocks, dest = layout(key)
    return dest


def with_ends(entries, key, smallest, top_value):
    longest = entries.shape.index(max(entries.shape))
    spots = []
    for shift in (0, 1):
        where = [jax.random.randint(jax.random.fold_in(key, axis), (), 0, length) for axis, length in enumerate(entries.shape)]
        where[longest] = (where[longest] + shift) % entries.shape[longest]
        spots.append(tuple(where))
    return entries.at[spots[0]].set(smallest).at[spots[1]].set(top_value)


def levels(rng, shape, shards, least, largest):
    def one(axis_at, shards_of):
        heights = jax.random.uniform(jax.random.fold_in(jax.random.fold_in(rng, 6), axis_at), (shards_of,), jnp.float32, least / len(shards), largest / len(shards))
        return jnp.repeat(jnp.exp(heights), shape[axis_at] // shards_of).reshape((-1,) + (1,) * (len(shape) - axis_at - 1))

    level = one(*shards[0])
    for cut in shards[1:]:
        level = level * one(*cut)
    return level


def noise(stream_key, shape, width, reach, pieces=(), kind=jnp.bfloat16):
    gain = levels(stream_key, shape, pieces, -0.22, 0.18) if pieces else 1.0
    drawn = jax.random.normal(stream_key, shape, jnp.float32) * width * gain
    return jnp.minimum(jnp.maximum(drawn, -reach), reach).astype(kind)


def setup_inputs(seed: int = 0, part: int = 0) -> dict:
    arg_keys = jax.random.split(jax.random.key(seed), 10)
    own_keys = jax.random.split(jax.random.fold_in(arg_keys[9], part), 10)
    return {
        "tokens": noise(own_keys[0], (ROWS, D), 1.0, 6.0, ((0, 8), (1, 2))),
        "norm_gain": jnp.clip(1.0 + 0.18 * jax.random.normal(arg_keys[1], (D,), jnp.float32), 0.099609375, 1.8984375).astype(jnp.bfloat16),
        "key_weight": noise(arg_keys[2], (D, KVW), D ** -0.5, 0.078125, ((0, 2), (1, 2))),
        "value_weight": noise(arg_keys[3], (D, KVW), D ** -0.5, 0.078125, ((0, 2), (1, 2))),
        "key_bias": noise(arg_keys[4], (KVW,), 0.5, 3.0, ((0, 2),)),
        "value_bias": noise(arg_keys[5], (KVW,), 0.5, 3.0, ((0, 2),)),
        "block_counts": draw_block_counts(jax.random.fold_in(jax.random.fold_in(arg_keys[9], part), 71), part),
        "positions": with_ends(jax.random.randint(own_keys[7], (ROWS,), 0, 32768), jax.random.fold_in(own_keys[7], 1), 0, 32767).astype(jnp.int32),
        "dest_slots": draw_dest_slots(jax.random.fold_in(jax.random.fold_in(arg_keys[9], part), 71), part),
    }


epsilon = 1e-05
rope_base = 1000000.0

def rotate(key_rows, positions, head_dim):
    row_count = key_rows.shape[0]
    head_view = key_rows.reshape(row_count, -1, head_dim)
    half_rot = head_dim // 4
    freq_index = jnp.arange(half_rot, dtype=jnp.float32)
    inverse = rope_base ** (-freq_index / half_rot)
    angles = positions.astype(jnp.float32)[:, None] * inverse[None, :]
    cosine = jnp.cos(angles)[:, None, :]
    sine_part = jnp.sin(angles)[:, None, :]
    first_half = head_view[..., :half_rot]
    second = head_view[..., half_rot:2 * half_rot]
    tail_dims = head_view[..., 2 * half_rot:]
    turned = jnp.concatenate([first_half * cosine - second * sine_part, second * cosine + first_half * sine_part, tail_dims], axis=-1)
    return turned.reshape(row_count, -1)

def reference(tokens, norm_gain, key_weight, value_weight, key_bias, value_bias, block_counts, positions, dest_slots):
    row_ids = jnp.arange(ROWS, dtype=jnp.int32)
    is_valid = (row_ids % TOK_DEV < BLOCK * block_counts[row_ids // TOK_DEV]) & (dest_slots >= 0)
    target = jnp.where(is_valid, dest_slots, OUT_ROWS).astype(jnp.int32)
    source = jnp.zeros((OUT_ROWS,), jnp.int32).at[target].set(row_ids, mode='drop')
    filled = jnp.zeros((OUT_ROWS,), jnp.float32).at[target].set(1.0, mode='drop')

    def one_block(begin_row):
        picked = lax.dynamic_slice_in_dim(source, begin_row, OWN_DEV)
        float_rows = tokens[picked].astype(jnp.float32)
        mean_square = lax.optimization_barrier(jnp.mean(float_rows * float_rows, axis=-1, keepdims=True))
        normed = (float_rows * lax.rsqrt(mean_square + epsilon) * norm_gain.astype(jnp.float32)).astype(jnp.bfloat16)
        key_rows = jnp.dot(normed, key_weight, preferred_element_type=jnp.float32) + key_bias.astype(jnp.float32)
        values = jnp.dot(normed, value_weight, preferred_element_type=jnp.float32) + value_bias.astype(jnp.float32)
        key_rows = rotate(key_rows, positions[picked], HEAD_DIM)
        row_mask = lax.dynamic_slice_in_dim(filled, begin_row, OWN_DEV)[:, None]
        return ((key_rows * row_mask).astype(jnp.bfloat16), (values * row_mask).astype(jnp.bfloat16))
    block_starts = jnp.arange(DEVS, dtype=jnp.int32) * OWN_DEV
    key_rows, values = lax.map(one_block, block_starts)
    return (key_rows.reshape(OUT_ROWS, KVW), values.reshape(OUT_ROWS, KVW))
```

```python
import functools

import jax
import jax.numpy as jnp
from jax import lax
from jax.experimental import pallas as pl
from jax.experimental.pallas import tpu as pltpu
from jax.sharding import PartitionSpec as P

HEAD_DIM = 128
BLOCK = 128
HOT_BLOCKS = 5
OWN_DEV = 256


epsilon = 1e-05
rope_base = 1000000.0
VMEM_BYTES = 48 * 1024 * 1024


def rotary_tables(positions):
    half_rot = HEAD_DIM // 4
    freq_index = jnp.arange(half_rot, dtype=jnp.float32)
    inverse = rope_base ** (-freq_index / half_rot)
    angles = positions.astype(jnp.float32)[:, None] * inverse[None, :]
    cosine = jnp.cos(angles)
    sine = jnp.sin(angles)
    rest = jnp.zeros((positions.shape[0], HEAD_DIM - 2 * half_rot), jnp.float32)
    straight = jnp.concatenate([cosine, cosine, rest + 1.0], axis=1)
    crossed = jnp.concatenate([-sine, sine, rest], axis=1)
    return straight, crossed


def norm_kernel(half_ref, own_ref, got_ref, gain_ref, out_ref):
    half = half_ref[0]
    width = own_ref.shape[1]
    own = own_ref[...].astype(jnp.float32)
    got = got_ref[...].astype(jnp.float32)
    total = jnp.sum(own * own, axis=1, keepdims=True) + jnp.sum(got * got, axis=1, keepdims=True)
    scale = lax.rsqrt(total / (2 * width) + epsilon)
    out_ref[:, :width] = (own * scale * gain_ref[half].astype(jnp.float32)).astype(jnp.bfloat16)
    out_ref[:, width:] = (got * scale * gain_ref[1 - half].astype(jnp.float32)).astype(jnp.bfloat16)


def normalize(half, own, got, norm_gain):
    rows, width = own.shape
    step = 128
    return pl.pallas_call(
        norm_kernel,
        out_shape=jax.ShapeDtypeStruct((rows, 2 * width), jnp.bfloat16),
        grid_spec=pltpu.PrefetchScalarGridSpec(
            num_scalar_prefetch=1,
            grid=(rows // step,),
            in_specs=[
                pl.BlockSpec((step, width), lambda i, half: (i, 0)),
                pl.BlockSpec((step, width), lambda i, half: (i, 0)),
                pl.BlockSpec((2, 1, width), lambda i, half: (0, 0, 0)),
            ],
            out_specs=pl.BlockSpec((step, 2 * width), lambda i, half: (i, 0)),
        ),
        compiler_params=pltpu.CompilerParams(vmem_limit_bytes=VMEM_BYTES),
        name="normalize",
    )(half.reshape(1), own, got, norm_gain.reshape(2, 1, width))


def near_kernel(place_ref, normed_ref, key_ref, value_ref, bias_ref, keys_ref, values_ref):
    rows = normed_ref[...]
    keys_ref[...] = (
        jnp.dot(rows, key_ref[...], preferred_element_type=jnp.float32) + bias_ref[0:1, :]
    )
    values_ref[...] = (
        jnp.dot(rows, value_ref[...], preferred_element_type=jnp.float32) + bias_ref[1:2, :]
    )


def near_part(place, normed, key_weight, value_weight, key_bias, value_bias):
    rows = normed.shape[0]
    depth, columns = key_weight.shape
    step = 128
    bias = jnp.stack([key_bias, value_bias]).astype(jnp.float32)
    out = jax.ShapeDtypeStruct((rows, columns), jnp.float32)
    return pl.pallas_call(
        near_kernel,
        out_shape=(out, out),
        grid_spec=pltpu.PrefetchScalarGridSpec(
            num_scalar_prefetch=1,
            grid=(rows // step,),
            in_specs=[
                pl.BlockSpec((step, depth), lambda i, place: (i, place[0])),
                pl.BlockSpec((depth, columns), lambda i, place: (0, 0)),
                pl.BlockSpec((depth, columns), lambda i, place: (0, 0)),
                pl.BlockSpec((2, columns), lambda i, place: (0, 0)),
            ],
            out_specs=(
                pl.BlockSpec((step, columns), lambda i, place: (i, 0)),
                pl.BlockSpec((step, columns), lambda i, place: (i, 0)),
            ),
        ),
        compiler_params=pltpu.CompilerParams(vmem_limit_bytes=VMEM_BYTES),
        name="near_part",
    )(place.reshape(1), normed, key_weight, value_weight, bias)


def far_kernel(turn, count, places_ref, normed_ref, near_ref, *refs):
    pieces = refs[:count]
    if turn:
        straight_ref, crossed_ref, pick_ref, out_ref = refs[count:]
    else:
        pick_ref, out_ref = refs[count:]
    total = near_ref[...]
    for index, piece in enumerate(pieces):
        depth = piece.shape[0]
        start = pl.multiple_of(places_ref[index] * depth, depth)
        total += jnp.dot(
            normed_ref[:, pl.ds(start, depth)], piece[...], preferred_element_type=jnp.float32
        )
    if turn:
        half_rot = HEAD_DIM // 4
        straight = straight_ref[...]
        crossed = crossed_ref[...]
        lane = lax.broadcasted_iota(jnp.int32, straight.shape, 1)
        heads = []
        for head in range(total.shape[1] // HEAD_DIM):
            part = total[:, head * HEAD_DIM : (head + 1) * HEAD_DIM]
            partner = jnp.where(
                lane < half_rot,
                pltpu.roll(part, HEAD_DIM - half_rot, 1),
                pltpu.roll(part, half_rot, 1),
            )
            heads.append(part * straight + partner * crossed)
        total = jnp.concatenate(heads, axis=1)
    rows = total.astype(jnp.bfloat16)
    out_ref[...] = jnp.dot(pick_ref[...], rows, preferred_element_type=jnp.float32).astype(
        jnp.bfloat16
    )


def far_part(places, normed, near, pieces, tables, pick):
    columns = near.shape[1]
    vmem = pl.BlockSpec(memory_space=pltpu.VMEM)
    operands = (normed, near, *pieces, *tables, pick)
    return pl.pallas_call(
        functools.partial(far_kernel, bool(tables), len(pieces)),
        out_shape=jax.ShapeDtypeStruct((pick.shape[0], columns), jnp.bfloat16),
        in_specs=[pl.BlockSpec(memory_space=pltpu.SMEM)] + [vmem] * len(operands),
        out_specs=vmem,
        compiler_params=pltpu.CompilerParams(vmem_limit_bytes=VMEM_BYTES),
        name="far_part",
    )(places, *operands)


def local(
    tokens,
    norm_gain,
    key_weight,
    value_weight,
    key_bias,
    value_bias,
    block_counts,
    positions,
    dest_slots,
):
    axes = ("rep", "fsdp")
    devices = lax.axis_size(axes)
    most_rows = (HOT_BLOCKS + 1) * (BLOCK // devices)
    capacity = devices * most_rows
    my_index = lax.axis_index(axes)
    rows, width = tokens.shape
    depth = key_weight.shape[0]
    shards = lax.axis_size("fsdp")
    half = lax.axis_index("tp")
    shard = lax.axis_index("fsdp")

    def place_of(first, size):
        which = first // width
        return (jnp.where(which == half, 0, width) + first % width) // size

    got = lax.ppermute(tokens, "tp", [(0, 1), (1, 0)])

    quarter = depth // 4
    relayed = (
        shards == 2
        and lax.axis_size("groups") == 2
        and lax.axis_size("rep") % 2 == 0
        and depth % 4 == 0
        and quarter % 128 == 0
    )
    if relayed:
        group = lax.axis_index("groups")
        odd = lax.axis_index("rep") % 2
        swap = [(0, 1), (1, 0)]
        across = [(i, i ^ 1) for i in range(lax.axis_size("rep"))]
        mine = 2 * group + odd
        last = 3 - mine
        far_first = (1 - shard) * depth

        def pieces_of(weight):
            own = lax.ppermute(
                lax.dynamic_slice_in_dim(weight, mine * quarter, quarter), "fsdp", swap
            )
            opposite = lax.ppermute(
                lax.dynamic_slice_in_dim(weight, last * quarter, quarter), "fsdp", swap
            )
            by_group = lax.ppermute(own, "groups", swap)
            by_rep = lax.ppermute(own, "rep", across)
            return own, by_group, by_rep, opposite

        numbers = (mine, 2 * (1 - group) + odd, 2 * group + 1 - odd, last)
        places = jnp.stack([place_of(far_first + n * quarter, quarter) for n in numbers])
        key_pieces = pieces_of(key_weight)
        value_pieces = pieces_of(value_weight)
    else:
        steps = range(1, shards)

        def pieces_of(weight):
            return tuple(
                lax.ppermute(weight, "fsdp", [(i, (i + k) % shards) for i in range(shards)])
                for k in steps
            )

        places = jnp.stack([place_of(((shard - k) % shards) * depth, depth) for k in steps])
        key_pieces = pieces_of(key_weight)
        value_pieces = pieces_of(value_weight)

    local_index = jnp.arange(rows, dtype=jnp.int32)
    is_valid = (local_index < BLOCK * block_counts[my_index]) & (dest_slots >= 0)
    owner_index = jnp.where(is_valid, dest_slots // OWN_DEV, -1)
    slot_local = jnp.where(is_valid, dest_slots % OWN_DEV, -1)
    onehot = (owner_index[:, None] == jnp.arange(devices, dtype=jnp.int32)[None, :]).astype(
        jnp.int32
    )
    rank_in_slot = jnp.sum((jnp.cumsum(onehot, axis=0) - 1) * onehot, axis=1)
    target = jnp.where(is_valid, owner_index * most_rows + rank_in_slot, capacity)
    hit = jnp.arange(capacity, dtype=jnp.int32)[:, None] == target[None, :]
    pick = hit.astype(jnp.bfloat16)
    marks = jnp.max(jnp.where(hit, slot_local[None, :], -1), axis=1).astype(jnp.bfloat16)
    got_marks = lax.all_to_all(marks, axes, split_axis=0, concat_axis=0, tiled=True)
    put = (
        jnp.arange(OWN_DEV, dtype=jnp.int32)[:, None] == got_marks.astype(jnp.int32)[None, :]
    ).astype(jnp.bfloat16)
    tables = rotary_tables(positions)

    normed = normalize(half, tokens, got, norm_gain)
    near_keys, near_values = near_part(
        place_of(shard * depth, depth), normed, key_weight, value_weight, key_bias, value_bias
    )
    outs = []
    for near, pieces, turn in (
        (near_keys, key_pieces, tables),
        (near_values, value_pieces, ()),
    ):
        send = far_part(places, normed, near, pieces, turn, pick)
        came = lax.all_to_all(send, axes, split_axis=0, concat_axis=0, tiled=True)
        outs.append(
            jnp.dot(put, came, preferred_element_type=jnp.float32).astype(jnp.bfloat16)
        )
    return tuple(outs)


def solution(mesh):
    return jax.shard_map(
        local,
        mesh=mesh,
        in_specs=(
            P(("groups", "rep", "fsdp"), "tp"),
            P(),
            P("fsdp", "tp"),
            P("fsdp", "tp"),
            P("tp"),
            P("tp"),
            P("groups"),
            P(("groups", "rep", "fsdp")),
            P(("groups", "rep", "fsdp")),
        ),
        out_specs=(P(("groups", "rep", "fsdp"), "tp"), P(("groups", "rep", "fsdp"), "tp")),
        check_vma=False,
    )
```

```python
import functools

import jax
import jax.numpy as jnp
from jax import lax
from jax.experimental import pallas as pl
from jax.experimental.pallas import tpu as pltpu
from jax.sharding import PartitionSpec as P

HEAD_DIM = 128
BLOCK = 128
HOT_BLOCKS = 5
OWN_DEV = 256


epsilon = 1e-05
rope_base = 1000000.0
VMEM_BYTES = 58 * 1024 * 1024
NEAR_STEP = 128
NEAR_CUTS = 4
NEAR_COST = 20_000_000_000
FAR_COST = 20_000_000_000


def ordered(*values):
    return lax.optimization_barrier(values)


def place_of(first, width):
    return jnp.where(first // width == lax.axis_index("tp"), 0, width) + first % width


def quarter_numbers():
    group = lax.axis_index("groups")
    odd = lax.rem(lax.axis_index("rep"), 2)
    return (2 * group + odd, 2 * (1 - group) + odd, 2 * group + 1 - odd, 3 - 2 * group - odd)


def far_places(relayed, depth, width):
    if relayed:
        return [number * (depth // 4) for number in quarter_numbers()]
    shards = lax.axis_size("fsdp")
    shard = lax.axis_index("fsdp")
    others = [lax.rem(shard + shards - k, shards) * depth for k in range(1, shards)]
    return [place_of(first, width) if depth != width else 0 for first in others]


def rotary_angles(positions):
    half_rot = HEAD_DIM // 4
    freq_index = jnp.arange(half_rot, dtype=jnp.float32)
    inverse = rope_base ** (-freq_index / half_rot)
    angles = inverse[:, None] * positions.astype(jnp.float32)[None, :]
    return jnp.cos(angles), jnp.sin(angles)


def cut_kernel(key_ref, value_ref, *refs):
    outs, sems = refs[:4], refs[4]
    quarter = outs[0].shape[0]
    mine = 2 * lax.axis_index("groups") + lax.rem(lax.axis_index("rep"), 2)
    copies = []
    for index, (source, which) in enumerate(
        ((key_ref, mine), (value_ref, mine), (key_ref, 3 - mine), (value_ref, 3 - mine))
    ):
        start = pl.multiple_of(which * quarter, quarter)
        copy = pltpu.make_async_copy(
            source.at[pl.ds(start, quarter), :], outs[index], sems.at[index]
        )
        copy.start()
        copies.append(copy)
    for copy in copies:
        copy.wait()


def cut_quarters(key_weight, value_weight):
    depth, columns = key_weight.shape
    piece = jax.ShapeDtypeStruct((depth // 4, columns), key_weight.dtype)
    return pl.pallas_call(
        cut_kernel,
        out_shape=(piece,) * 4,
        in_specs=[pl.BlockSpec(memory_space=pl.ANY)] * 2,
        out_specs=(pl.BlockSpec(memory_space=pltpu.VMEM),) * 4,
        scratch_shapes=[pltpu.SemaphoreType.DMA((4,))],
        compiler_params=pltpu.CompilerParams(vmem_limit_bytes=VMEM_BYTES),
        name="cut_quarters",
    )(key_weight, value_weight)


def near_kernel(whole, cuts, *refs):
    own_refs, got_refs = refs[:cuts], refs[cuts : 2 * cuts]
    gain_ref = refs[2 * cuts]
    key_refs, value_refs = refs[2 * cuts + 1 : 3 * cuts + 1], refs[3 * cuts + 1 : 4 * cuts + 1]
    key_bias_ref, value_bias_ref, keys_ref, values_ref, far_ref, normed_ref = refs[4 * cuts + 1 :]
    size, part_width = own_refs[0].shape
    width = cuts * part_width
    part_depth = key_refs[0].shape[0]
    depth = cuts * part_depth
    half = lax.axis_index("tp")
    lanes = 128
    squares = jnp.zeros((size, lanes), jnp.float32)
    for source in own_refs + got_refs:
        for first in range(0, part_width, lanes):
            part = source[:, first : first + lanes].astype(jnp.float32)
            squares += part * part
    total = jnp.sum(squares, axis=1, keepdims=True)
    scale = jnp.broadcast_to(lax.rsqrt(total / (2 * width) + epsilon), (size, lanes))
    for sources, side, which in ((own_refs, 0, half), (got_refs, width, 1 - half)):
        gain = gain_ref[pl.ds(pl.multiple_of(which * width, width), width)].astype(jnp.float32)
        gain = gain.reshape(1, width)
        for first in range(0, width, lanes):
            inner = first % part_width
            part = sources[first // part_width][:, inner : inner + lanes].astype(jnp.float32)
            normed_ref[:, side + first : side + first + lanes] = (
                part * scale * gain[:, first : first + lanes]
            ).astype(jnp.bfloat16)
    near_first = pl.multiple_of(place_of(lax.axis_index("fsdp") * depth, width), depth)
    for pieces, bias_ref, out_ref in (
        (key_refs, key_bias_ref, keys_ref),
        (value_refs, value_bias_ref, values_ref),
    ):
        sums = jnp.broadcast_to(
            bias_ref[...].astype(jnp.float32).reshape(1, out_ref.shape[1]), out_ref.shape
        )
        for index, piece in enumerate(pieces):
            start = pl.multiple_of(near_first + index * part_depth, part_depth)
            sums += jnp.dot(
                normed_ref[:, pl.ds(start, part_depth)],
                piece[...],
                preferred_element_type=jnp.float32,
            )
        out_ref[...] = sums
    if whole:
        far_ref[...] = normed_ref[...]
    else:
        far_ref[...] = normed_ref[:, pl.ds(pl.multiple_of(width - near_first, width), width)]


def near_part(own, got, norm_gain, key_weight, value_weight, key_bias, value_bias):
    rows, width = own.shape
    depth, columns = key_weight.shape
    whole = depth != width
    kept = 2 * width if whole else width
    cuts = NEAR_CUTS if depth % (128 * NEAR_CUTS) == 0 else 1
    step = NEAR_STEP
    sums = jax.ShapeDtypeStruct((rows, columns), jnp.float32)
    row_blocks = [
        pl.BlockSpec((step, width // cuts), lambda i, c=c: (i, c)) for c in range(cuts)
    ]
    weight_blocks = [
        pl.BlockSpec((depth // cuts, columns), lambda i, c=c: (c, 0)) for c in range(cuts)
    ]
    return pl.pallas_call(
        functools.partial(near_kernel, whole, cuts),
        out_shape=(sums, sums, jax.ShapeDtypeStruct((rows, kept), jnp.bfloat16)),
        grid=(rows // step,),
        in_specs=[
            *row_blocks,
            *row_blocks,
            pl.BlockSpec((2 * width,), lambda i: (0,)),
            *weight_blocks,
            *weight_blocks,
            pl.BlockSpec((columns,), lambda i: (0,)),
            pl.BlockSpec((columns,), lambda i: (0,)),
        ],
        out_specs=(
            pl.BlockSpec((step, columns), lambda i: (i, 0)),
            pl.BlockSpec((step, columns), lambda i: (i, 0)),
            pl.BlockSpec((step, kept), lambda i: (i, 0)),
        ),
        scratch_shapes=[pltpu.VMEM((step, 2 * width), jnp.bfloat16)],
        compiler_params=pltpu.CompilerParams(vmem_limit_bytes=VMEM_BYTES),
        cost_estimate=pl.CostEstimate(
            flops=NEAR_COST,
            bytes_accessed=6 * rows * width + 4 * depth * columns,
            transcendentals=0,
        ),
        name="near_part",
    )(
        *[own] * cuts,
        *[got] * cuts,
        norm_gain,
        *[key_weight] * cuts,
        *[value_weight] * cuts,
        key_bias,
        value_bias,
    )


def turned(total, straight, crossed):
    half_rot = HEAD_DIM // 4
    lane = lax.broadcasted_iota(jnp.int32, straight.shape, 1)
    heads = []
    for head in range(total.shape[1] // HEAD_DIM):
        part = total[:, head * HEAD_DIM : (head + 1) * HEAD_DIM]
        partner = jnp.where(
            lane < half_rot,
            pltpu.roll(part, HEAD_DIM - half_rot, 1),
            pltpu.roll(part, half_rot, 1),
        )
        heads.append(part * straight + partner * crossed)
    return jnp.concatenate(heads, axis=1)


def far_kernel(relayed, half_width, turn, extra, count, *refs):
    normed_ref, near_ref = refs[:2]
    pieces = refs[2 : 2 + count]
    rest = list(refs[2 + count :])
    rows_ref = rest.pop()
    out_ref = rest.pop()
    rest.pop()
    if turn:
        straight_ref, crossed_ref = rest.pop(0), rest.pop(0)
    pick_ref = rest.pop(0)
    step, total_steps = pl.program_id(0), pl.num_programs(0)
    size = near_ref.shape[0]
    total = near_ref[...]
    depth = pieces[0].shape[0]
    places = far_places(relayed, depth * 4 if relayed else depth, half_width)
    for piece, start in zip(pieces, places):
        start = pl.multiple_of(start, depth)
        total += jnp.dot(
            normed_ref[:, pl.ds(start, depth)], piece[...], preferred_element_type=jnp.float32
        )
    if turn:
        total = turned(total, straight_ref[...], crossed_ref[...])
    rows_ref[pl.ds(pl.multiple_of(step * size, size), size), :] = total.astype(jnp.bfloat16)

    @pl.when(step == total_steps - 1)
    def _():
        laid = jnp.dot(pick_ref[...], rows_ref[...], preferred_element_type=jnp.float32).astype(
            jnp.bfloat16
        )
        if extra:
            extra_ref = rest.pop(0)
            owners, tall, columns = out_ref.shape
            most_rows = tall - extra
            out_ref[:, :most_rows, :] = laid.reshape(owners, most_rows, columns)
            out_ref[:, most_rows:, :] = extra_ref[...]
        else:
            out_ref[...] = laid


def far_part(relayed, width, normed, near, pieces, tables, pick, extra, after):
    rows, columns = near.shape
    step = 320
    operands = [normed, near, *pieces, *tables, pick]
    specs = [
        pl.BlockSpec((step, normed.shape[1]), lambda i: (i, 0)),
        pl.BlockSpec((step, columns), lambda i: (i, 0)),
        *[pl.BlockSpec(piece.shape, lambda i: (0, 0)) for piece in pieces],
        *[pl.BlockSpec((step, HEAD_DIM), lambda i: (i, 0)) for _ in tables],
        pl.BlockSpec(pick.shape, lambda i: (0, 0)),
    ]
    tall = 0
    if extra is None:
        shape = (pick.shape[0], columns)
    else:
        owners, tall, _ = extra.shape
        shape = (owners, pick.shape[0] // owners + tall, columns)
        operands.append(extra)
        specs.append(pl.BlockSpec(extra.shape, lambda i: (0, 0, 0)))
    operands.append(after)
    specs.append(pl.BlockSpec(memory_space=pl.ANY))
    return pl.pallas_call(
        functools.partial(far_kernel, relayed, width, bool(tables), tall, len(pieces)),
        out_shape=jax.ShapeDtypeStruct(shape, jnp.bfloat16),
        grid=(rows // step,),
        in_specs=specs,
        out_specs=pl.BlockSpec(shape, lambda i: (0,) * len(shape)),
        scratch_shapes=[pltpu.VMEM((rows, columns), jnp.bfloat16)],
        compiler_params=pltpu.CompilerParams(vmem_limit_bytes=VMEM_BYTES),
        cost_estimate=pl.CostEstimate(
            flops=FAR_COST,
            bytes_accessed=2 * rows * normed.shape[1] + 6 * rows * columns,
            transcendentals=0,
        ),
        name="far_part",
    )(*operands)


def route_kernel(most_rows, counts_ref, dest_ref, cosine_ref, sine_ref, *refs):
    pick_ref, marks_ref, straight_ref, crossed_ref = refs[1:]
    me = lax.axis_index("rep") * lax.axis_size("fsdp") + lax.axis_index("fsdp")
    devices = marks_ref.shape[0]
    rows = dest_ref.shape[0]
    dest = dest_ref[...].reshape(1, rows)
    row = lax.broadcasted_iota(jnp.int32, (1, rows), 1)
    valid = (row < BLOCK * counts_ref[me]) & (dest >= 0)
    owner = jnp.where(valid, lax.div(dest, OWN_DEV), -1)
    slot = jnp.where(valid, lax.rem(dest, OWN_DEV), -1)
    tall = -(-devices // 16) * 16
    to_owner = lax.broadcasted_iota(jnp.int32, (tall, rows), 0) == owner
    ones = jnp.where(to_owner, 1.0, 0.0)
    earlier = jnp.where(
        lax.broadcasted_iota(jnp.int32, (rows, rows), 0)
        < lax.broadcasted_iota(jnp.int32, (rows, rows), 1),
        1.0,
        0.0,
    ).astype(jnp.bfloat16)
    before = jnp.dot(ones.astype(jnp.bfloat16), earlier, preferred_element_type=jnp.float32)
    rank = jnp.sum(ones * before, axis=0, keepdims=True).astype(jnp.int32)
    capacity = pick_ref.shape[0]
    target = jnp.where(valid, owner * most_rows + rank, capacity)
    pick_ref[...] = jnp.where(
        lax.broadcasted_iota(jnp.int32, (capacity, rows), 0) == target, 1.0, 0.0
    ).astype(jnp.bfloat16)
    at_rank = jnp.where(
        (lax.broadcasted_iota(jnp.int32, (marks_ref.shape[2], rows), 0) == rank) & valid, 1.0, 0.0
    ).astype(jnp.bfloat16)
    slots = jnp.where(to_owner, (slot + 1).astype(jnp.float32), 0.0).astype(jnp.bfloat16)
    marks = lax.dot_general(
        slots, at_rank, (((1,), (1,)), ((), ())), preferred_element_type=jnp.float32
    )
    marks = marks[:devices] - 1.0
    marks_ref[...] = jnp.broadcast_to(marks[:, None, :], marks_ref.shape).astype(jnp.bfloat16)
    cosine, sine = cosine_ref[...], sine_ref[...]
    rest = jnp.zeros((HEAD_DIM - 2 * cosine.shape[0], rows), jnp.float32)
    straight_ref[...] = jnp.concatenate([cosine, cosine, rest + 1.0], axis=0).T
    crossed_ref[...] = jnp.concatenate([-sine, sine, rest], axis=0).T


def route(block_counts, dest_slots, angles, devices, most_rows, columns, after):
    rows = dest_slots.shape[0]
    vmem = pl.BlockSpec(memory_space=pltpu.VMEM)
    return pl.pallas_call(
        functools.partial(route_kernel, most_rows),
        out_shape=(
            jax.ShapeDtypeStruct((devices * most_rows, rows), jnp.bfloat16),
            jax.ShapeDtypeStruct((devices, 16, columns), jnp.bfloat16),
            jax.ShapeDtypeStruct((rows, HEAD_DIM), jnp.float32),
            jax.ShapeDtypeStruct((rows, HEAD_DIM), jnp.float32),
        ),
        in_specs=[
            pl.BlockSpec(memory_space=pltpu.SMEM),
            vmem,
            vmem,
            vmem,
            pl.BlockSpec(memory_space=pl.ANY),
        ],
        out_specs=(vmem,) * 4,
        compiler_params=pltpu.CompilerParams(vmem_limit_bytes=VMEM_BYTES),
        name="route",
    )(block_counts, dest_slots, *angles, after)


def local(
    tokens,
    norm_gain,
    key_weight,
    value_weight,
    key_bias,
    value_bias,
    block_counts,
    positions,
    dest_slots,
):
    axes = ("rep", "fsdp")
    devices = lax.axis_size(axes)
    most_rows = (HOT_BLOCKS + 1) * (BLOCK // devices)
    capacity = devices * most_rows
    rows, width = tokens.shape
    depth = key_weight.shape[0]
    shards = lax.axis_size("fsdp")

    def exchange(rows_by_owner):
        return lax.all_to_all(rows_by_owner, axes, split_axis=0, concat_axis=0, tiled=True)

    got = lax.ppermute(tokens, "tp", [(0, 1), (1, 0)])

    near_keys, near_values, normed = near_part(
        tokens,
        got,
        norm_gain,
        key_weight,
        value_weight,
        key_bias,
        value_bias,
    )
    quarter = depth // 4
    relayed = (
        shards == 2
        and lax.axis_size("groups") == 2
        and lax.axis_size("rep") % 2 == 0
        and depth % 4 == 0
        and quarter % 128 == 0
    )
    if relayed:
        swap = [(0, 1), (1, 0)]
        across = [(i, i ^ 1) for i in range(lax.axis_size("rep"))]
        key_own, value_own, key_last, value_last = (
            lax.ppermute(piece, "fsdp", swap) for piece in cut_quarters(key_weight, value_weight)
        )

        key_own, near_values = ordered(key_own, near_values)

        def pieces_of(own, opposite):
            by_group = lax.ppermute(own, "groups", swap)
            by_rep = lax.ppermute(own, "rep", across)
            return own, by_group, by_rep, opposite

        key_pieces = pieces_of(key_own, key_last)
        value_pieces = pieces_of(value_own, value_last)
    else:
        steps = range(1, shards)

        def pieces_of(weight):
            return tuple(
                lax.ppermute(weight, "fsdp", [(i, (i + k) % shards) for i in range(shards)])
                for k in steps
            )

        key_pieces = pieces_of(key_weight)
        value_pieces = pieces_of(value_weight)

    columns = key_weight.shape[1]
    inline = most_rows % 16 == 0 and most_rows <= columns
    pick, marks, *tables = route(
        block_counts,
        dest_slots,
        rotary_angles(positions),
        devices,
        most_rows,
        columns,
        near_values,
    )
    if not inline:
        got_marks = exchange(marks[:, 0, :most_rows].reshape(capacity))
    send_keys = far_part(
        relayed,
        width,
        normed,
        near_keys,
        key_pieces,
        tables,
        pick,
        marks if inline else None,
        value_pieces[0],
    )
    came_keys = exchange(send_keys)
    send_values = far_part(
        relayed, width, normed, near_values, value_pieces, (), pick, None, send_keys
    )
    came_values = exchange(send_values)
    if inline:
        got_marks = came_keys[:, most_rows, :most_rows].reshape(capacity)
        came_keys = came_keys[:, :most_rows].reshape(capacity, columns)
    put = (
        jnp.arange(OWN_DEV, dtype=jnp.int32)[:, None] == got_marks.astype(jnp.int32)[None, :]
    ).astype(jnp.bfloat16)
    return tuple(
        jnp.dot(put, came, preferred_element_type=jnp.float32).astype(jnp.bfloat16)
        for came in (came_keys, came_values)
    )


def solution(mesh):
    return jax.shard_map(
        local,
        mesh=mesh,
        in_specs=(
            P(("groups", "rep", "fsdp"), "tp"),
            P(),
            P("fsdp", "tp"),
            P("fsdp", "tp"),
            P("tp"),
            P("tp"),
            P("groups"),
            P(("groups", "rep", "fsdp")),
            P(("groups", "rep", "fsdp")),
        ),
        out_specs=(P(("groups", "rep", "fsdp"), "tp"), P(("groups", "rep", "fsdp"), "tp")),
        check_vma=False,
    )
```

```python
import functools

import jax
import jax.numpy as jnp
from jax import lax
from jax.experimental import pallas as pl
from jax.experimental.pallas import tpu as pltpu
from jax.sharding import PartitionSpec as P

HEAD_DIM = 128
BLOCK = 128
HOT_BLOCKS = 5
OWN_DEV = 256


epsilon = 1e-05
rope_base = 1000000.0
VMEM_BYTES = 62 * 1024 * 1024
NEAR_STEP = 128
NEAR_COST = 20_000_000_000
FAR_COST = 20_000_000_000


def ordered(*values):
    return lax.optimization_barrier(values)


def group_index():
    return lax.axis_index("rep") * lax.axis_size("fsdp") + lax.axis_index("fsdp")


def quarter_numbers():
    group = lax.axis_index("groups")
    odd = lax.rem(lax.axis_index("rep"), 2)
    return (2 * group + odd, 2 * (1 - group) + odd, 2 * group + 1 - odd, 3 - 2 * group - odd)


def far_places(relayed, depth):
    shards = lax.axis_size("fsdp")
    shard = lax.axis_index("fsdp")
    if relayed:
        return [(1 - shard) * depth + number * (depth // 4) for number in quarter_numbers()]
    return [lax.rem(shard + shards - k, shards) * depth for k in range(1, shards)]


def rotary_angles(positions):
    half_rot = HEAD_DIM // 4
    freq_index = jnp.arange(half_rot, dtype=jnp.float32)
    inverse = rope_base ** (-freq_index / half_rot)
    angles = inverse[:, None] * positions.astype(jnp.float32)[None, :]
    return jnp.cos(angles), jnp.sin(angles)


def cut_kernel(key_ref, value_ref, *refs):
    outs, sems = refs[:4], refs[4]
    quarter = outs[0].shape[0]
    mine = 2 * lax.axis_index("groups") + lax.rem(lax.axis_index("rep"), 2)
    copies = []
    for index, (source, which) in enumerate(
        ((key_ref, mine), (value_ref, mine), (key_ref, 3 - mine), (value_ref, 3 - mine))
    ):
        start = pl.multiple_of(which * quarter, quarter)
        copy = pltpu.make_async_copy(
            source.at[pl.ds(start, quarter), :], outs[index], sems.at[index]
        )
        copy.start()
        copies.append(copy)
    for copy in copies:
        copy.wait()


def cut_quarters(key_weight, value_weight):
    depth, columns = key_weight.shape
    piece = jax.ShapeDtypeStruct((depth // 4, columns), key_weight.dtype)
    return pl.pallas_call(
        cut_kernel,
        out_shape=(piece,) * 4,
        in_specs=[pl.BlockSpec(memory_space=pl.ANY)] * 2,
        out_specs=(pl.BlockSpec(memory_space=pltpu.VMEM),) * 4,
        scratch_shapes=[pltpu.SemaphoreType.DMA((4,))],
        compiler_params=pltpu.CompilerParams(vmem_limit_bytes=VMEM_BYTES),
        name="cut_quarters",
    )(key_weight, value_weight)


def near_kernel(
    own_ref,
    got_ref,
    key_ref,
    value_ref,
    gain_ref,
    key_bias_ref,
    value_bias_ref,
    keys_ref,
    values_ref,
    scale_ref,
    own_buf,
    got_buf,
    key_buf,
    value_buf,
    normed_ref,
    key_sum,
    value_sum,
    scale_buf,
    sems,
):
    rows, width = own_ref.shape
    depth = key_ref.shape[0]
    size = NEAR_STEP
    blocks = rows // size

    def read(index):
        if index == blocks:
            pairs = ((key_ref, key_buf), (value_ref, value_buf))
        else:
            here = pl.ds(index * size, size)
            pairs = (
                (own_ref.at[here, :], own_buf.at[here, :]),
                (got_ref.at[here, :], got_buf.at[here, :]),
            )
        return [
            pltpu.make_async_copy(source, buf, sems.at[side, index])
            for side, (source, buf) in enumerate(pairs)
        ]

    def start(index):
        if index <= blocks:
            for copy in read(index):
                copy.start()

    start(0)
    start(1)
    lanes = 128
    near_first = lax.axis_index("fsdp") * depth
    side = near_first // width
    gain = gain_ref[pl.ds(pl.multiple_of(side * width, width), width)]
    gain = gain.astype(jnp.float32).reshape(1, width)
    writes = []
    for index in range(blocks):
        for copy in read(index):
            copy.wait()
        start(index + 2)
        here = pl.ds(index * size, size)
        squares = jnp.zeros((size, lanes), jnp.float32)
        for source in (own_buf, got_buf):
            for first in range(0, width, lanes):
                part = source[here, first : first + lanes].astype(jnp.float32)
                squares += part * part
        total = jnp.sum(squares, axis=1, keepdims=True)
        scale = jnp.broadcast_to(lax.rsqrt(total / (2 * width) + epsilon), (size, lanes))
        scale_buf[here, :] = scale
        for source, is_near in (
            (own_buf, side == lax.axis_index("tp")),
            (got_buf, side != lax.axis_index("tp")),
        ):

            @pl.when(is_near)
            def _(source=source, here=here, scale=scale):
                for first in range(0, width, lanes):
                    part = source[here, first : first + lanes].astype(jnp.float32)
                    normed_ref[here, first : first + lanes] = (
                        part * scale * gain[:, first : first + lanes]
                    ).astype(jnp.bfloat16)

    write = pltpu.make_async_copy(scale_buf, scale_ref, sems.at[2, 0])
    write.start()
    writes.append(write)
    for copy in read(blocks):
        copy.wait()
    for weight, bias_ref, sum_ref, out_ref in (
        (key_buf, key_bias_ref, key_sum, keys_ref),
        (value_buf, value_bias_ref, value_sum, values_ref),
    ):
        bias = bias_ref[...].astype(jnp.float32).reshape(1, sum_ref.shape[1])
        near = normed_ref[:, pl.ds(pl.multiple_of(near_first % width, depth), depth)]
        sum_ref[...] = jnp.dot(near, weight[...], preferred_element_type=jnp.float32) + bias
        write = pltpu.make_async_copy(sum_ref, out_ref, sems.at[2, len(writes)])
        write.start()
        writes.append(write)
    for write in writes:
        write.wait()


def near_part(own, got, norm_gain, key_weight, value_weight, key_bias, value_bias):
    rows, width = own.shape
    depth, columns = key_weight.shape
    sums = jax.ShapeDtypeStruct((rows, columns), jnp.float32)
    vmem = pl.BlockSpec(memory_space=pltpu.VMEM)
    anywhere = pl.BlockSpec(memory_space=pl.ANY)
    return pl.pallas_call(
        near_kernel,
        out_shape=(sums, sums, jax.ShapeDtypeStruct((rows, 128), jnp.float32)),
        in_specs=[anywhere] * 4 + [vmem] * 3,
        out_specs=(anywhere,) * 3,
        scratch_shapes=[
            pltpu.VMEM((rows, width), jnp.bfloat16),
            pltpu.VMEM((rows, width), jnp.bfloat16),
            pltpu.VMEM((depth, columns), jnp.bfloat16),
            pltpu.VMEM((depth, columns), jnp.bfloat16),
            pltpu.VMEM((rows, width), jnp.bfloat16),
            pltpu.VMEM((rows, columns), jnp.float32),
            pltpu.VMEM((rows, columns), jnp.float32),
            pltpu.VMEM((rows, 128), jnp.float32),
            pltpu.SemaphoreType.DMA((3, rows // NEAR_STEP + 1)),
        ],
        compiler_params=pltpu.CompilerParams(vmem_limit_bytes=VMEM_BYTES),
        cost_estimate=pl.CostEstimate(
            flops=NEAR_COST,
            bytes_accessed=6 * rows * width + 4 * depth * columns,
            transcendentals=0,
        ),
        name="near_part",
    )(own, got, key_weight, value_weight, norm_gain, key_bias, value_bias)


def turned(total, cosine, sine):
    half_rot, rows = cosine.shape
    rest = jnp.zeros((HEAD_DIM - 2 * half_rot, rows), jnp.float32)
    straight = jnp.concatenate([cosine, cosine, rest + 1.0], axis=0).T
    crossed = jnp.concatenate([-sine, sine, rest], axis=0).T
    lane = lax.broadcasted_iota(jnp.int32, straight.shape, 1)
    heads = []
    for head in range(total.shape[1] // HEAD_DIM):
        part = total[:, head * HEAD_DIM : (head + 1) * HEAD_DIM]
        partner = jnp.where(
            lane < half_rot,
            pltpu.roll(part, HEAD_DIM - half_rot, 1),
            pltpu.roll(part, half_rot, 1),
        )
        heads.append(part * straight + partner * crossed)
    return jnp.concatenate(heads, axis=1)


def picked(target_ref, first, size, rows):
    target = target_ref[0:1, :]
    line = lax.broadcasted_iota(jnp.int32, (size, target.shape[1]), 0) + first
    pick = jnp.where(line == target, 1.0, 0.0).astype(jnp.bfloat16)
    return jnp.dot(pick, rows, preferred_element_type=jnp.float32).astype(jnp.bfloat16)


def far_kernel(relayed, turn, extra, count, outs, *refs):
    own_ref, got_ref, near_ref, scale_ref = refs[:4]
    pieces = refs[4 : 4 + count]
    scratch = refs[-2 * count - 5 :]
    part_bufs, piece_bufs = scratch[:count], scratch[count : 2 * count]
    near_buf, scale_buf, gain_buf, normed_buf, sems = scratch[2 * count :]
    rest = list(refs[4 + count : -outs - 1 - len(scratch)])
    out_refs = refs[-outs - len(scratch) : -len(scratch)]
    depth = pieces[0].shape[0]
    width = own_ref.shape[1]
    places = far_places(relayed, depth * 4 if relayed else depth)
    lanes = 128
    near_copies = (
        pltpu.make_async_copy(near_ref, near_buf, sems.at[0, count]),
        pltpu.make_async_copy(scale_ref, scale_buf, sems.at[1, count]),
    )

    def part_copy(source, index):
        first = pl.multiple_of(places[index] % width, lanes)
        return pltpu.make_async_copy(
            source.at[:, pl.ds(first, depth)], part_bufs[index], sems.at[0, index]
        )

    def piece_copy(index):
        return pltpu.make_async_copy(pieces[index], piece_bufs[index], sems.at[1, index])

    for copy in near_copies:
        copy.start()
    for index in range(count):
        is_own = places[index] // width == lax.axis_index("tp")

        @pl.when(is_own)
        def _(index=index):
            part_copy(own_ref, index).start()

        @pl.when(jnp.logical_not(is_own))
        def _(index=index):
            part_copy(got_ref, index).start()

        piece_copy(index).start()
    gain_ref = rest.pop(0)
    gain_buf[...] = gain_ref[...].astype(jnp.float32).reshape(1, 2 * width)
    for copy in near_copies:
        copy.wait()
    total = near_buf[...]
    for index in range(count):
        part_copy(own_ref, index).wait()
        for first in range(0, depth, lanes):
            here = slice(first, first + lanes)
            gain = gain_buf[:, pl.ds(pl.multiple_of(places[index] + first, lanes), lanes)]
            part = part_bufs[index][:, here].astype(jnp.float32)
            normed_buf[:, here] = (part * scale_buf[...] * gain).astype(jnp.bfloat16)
        piece_copy(index).wait()
        total += jnp.dot(
            normed_buf[...], piece_bufs[index][...], preferred_element_type=jnp.float32
        )
    if turn:
        total = turned(total, rest.pop(0)[...], rest.pop(0)[...])
    target_ref = rest.pop(0)
    total = total.astype(jnp.bfloat16)
    if outs > 1:
        me = group_index()
        for other, out_ref in enumerate(out_refs):
            size = out_ref.shape[0]
            out_ref[...] = picked(target_ref, lax.bitwise_xor(me, other) * size, size, total)
    elif extra:
        extra_ref = rest.pop(0)
        owners, tall, columns = out_refs[0].shape
        most_rows = tall - extra
        laid = picked(target_ref, 0, owners * most_rows, total)
        out_refs[0][:, :most_rows, :] = laid.reshape(owners, most_rows, columns)
        out_refs[0][:, most_rows:, :] = extra_ref[...]
    else:
        out_refs[0][...] = picked(target_ref, 0, out_refs[0].shape[0], total)


def far_part(
    relayed, rows_of, norm_gain, near, scale, pieces, angles, target, capacity, extra, outs, after
):
    rows, columns = near.shape
    depth = pieces[0].shape[0]
    count = len(pieces)
    operands = [norm_gain, *angles, target]
    tall = 0
    if extra is None:
        shape = (capacity // outs, columns)
    else:
        owners, tall, _ = extra.shape
        shape = (owners, capacity // owners + tall, columns)
        operands.append(extra)
    vmem = pl.BlockSpec(memory_space=pltpu.VMEM)
    anywhere = pl.BlockSpec(memory_space=pl.ANY)
    return pl.pallas_call(
        functools.partial(far_kernel, relayed, bool(angles), tall, count, outs),
        out_shape=(jax.ShapeDtypeStruct(shape, jnp.bfloat16),) * outs,
        in_specs=[anywhere] * (4 + count) + [vmem] * len(operands) + [anywhere],
        out_specs=(vmem,) * outs,
        scratch_shapes=[
            *[pltpu.VMEM((rows, depth), jnp.bfloat16) for _ in pieces],
            *[pltpu.VMEM((depth, columns), jnp.bfloat16) for _ in pieces],
            pltpu.VMEM((rows, columns), jnp.float32),
            pltpu.VMEM(scale.shape, jnp.float32),
            pltpu.VMEM((1, norm_gain.shape[0]), jnp.float32),
            pltpu.VMEM((rows, depth), jnp.bfloat16),
            pltpu.SemaphoreType.DMA((2, count + 1)),
        ],
        compiler_params=pltpu.CompilerParams(vmem_limit_bytes=VMEM_BYTES),
        cost_estimate=pl.CostEstimate(
            flops=FAR_COST,
            bytes_accessed=12 * rows * columns,
            transcendentals=0,
        ),
        name="far_part",
    )(*rows_of, near, scale, *pieces, *operands, after)


def route_kernel(most_rows, counts_ref, dest_ref, after_ref, target_ref, marks_ref):
    me = group_index()
    devices = marks_ref.shape[0]
    rows = dest_ref.shape[0]
    dest = dest_ref[...].reshape(1, rows)
    row = lax.broadcasted_iota(jnp.int32, (1, rows), 1)
    valid = (row < BLOCK * counts_ref[me]) & (dest >= 0)
    owner = jnp.where(valid, lax.div(dest, OWN_DEV), -1)
    slot = jnp.where(valid, lax.rem(dest, OWN_DEV), -1)
    tall = -(-devices // 16) * 16
    to_owner = lax.broadcasted_iota(jnp.int32, (tall, rows), 0) == owner
    ones = jnp.where(to_owner, 1.0, 0.0)
    earlier = jnp.where(
        lax.broadcasted_iota(jnp.int32, (rows, rows), 0)
        < lax.broadcasted_iota(jnp.int32, (rows, rows), 1),
        1.0,
        0.0,
    ).astype(jnp.bfloat16)
    before = jnp.dot(ones.astype(jnp.bfloat16), earlier, preferred_element_type=jnp.float32)
    rank = jnp.sum(ones * before, axis=0, keepdims=True).astype(jnp.int32)
    target = jnp.where(valid, owner * most_rows + rank, devices * most_rows)
    target_ref[...] = jnp.broadcast_to(target, target_ref.shape)
    at_rank = jnp.where(
        (lax.broadcasted_iota(jnp.int32, (marks_ref.shape[2], rows), 0) == rank) & valid, 1.0, 0.0
    ).astype(jnp.bfloat16)
    slots = jnp.where(to_owner, (slot + 1).astype(jnp.float32), 0.0).astype(jnp.bfloat16)
    marks = lax.dot_general(
        slots, at_rank, (((1,), (1,)), ((), ())), preferred_element_type=jnp.float32
    )
    marks = marks[:devices] - 1.0
    marks_ref[...] = jnp.broadcast_to(marks[:, None, :], marks_ref.shape).astype(jnp.bfloat16)


def route(block_counts, dest_slots, devices, most_rows, columns, after):
    rows = dest_slots.shape[0]
    vmem = pl.BlockSpec(memory_space=pltpu.VMEM)
    return pl.pallas_call(
        functools.partial(route_kernel, most_rows),
        out_shape=(
            jax.ShapeDtypeStruct((8, rows), jnp.int32),
            jax.ShapeDtypeStruct((devices, 16, columns), jnp.bfloat16),
        ),
        in_specs=[
            pl.BlockSpec(memory_space=pltpu.SMEM),
            vmem,
            pl.BlockSpec(memory_space=pl.ANY),
        ],
        out_specs=(vmem,) * 2,
        compiler_params=pltpu.CompilerParams(vmem_limit_bytes=VMEM_BYTES),
        name="route",
    )(block_counts, dest_slots, after)


def place_kernel(came_ref, put_ref, out_ref):
    devices, tall, columns = came_ref.shape
    most_rows = tall - 16
    owned = out_ref.shape[0]
    total = jnp.zeros(out_ref.shape, jnp.float32)
    slot = lax.broadcasted_iota(jnp.int32, (owned, most_rows), 0)
    me = group_index()
    for other in range(devices):
        source = lax.bitwise_xor(me, other)
        marks = came_ref[source, most_rows:, :].astype(jnp.float32)[0:1, :most_rows]
        put = jnp.where(slot == marks.astype(jnp.int32), 1.0, 0.0).astype(jnp.bfloat16)
        put_ref[other, :, :most_rows] = put
        total += jnp.dot(put, came_ref[source, :most_rows, :], preferred_element_type=jnp.float32)
    out_ref[...] = total.astype(jnp.bfloat16)


def place_keys(came):
    devices, tall, columns = came.shape
    vmem = pl.BlockSpec(memory_space=pltpu.VMEM)
    return pl.pallas_call(
        place_kernel,
        out_shape=(
            jax.ShapeDtypeStruct((devices, OWN_DEV, 128), jnp.bfloat16),
            jax.ShapeDtypeStruct((OWN_DEV, columns), jnp.bfloat16),
        ),
        in_specs=[vmem],
        out_specs=(vmem,) * 2,
        compiler_params=pltpu.CompilerParams(vmem_limit_bytes=VMEM_BYTES),
        name="place_keys",
    )(came)


def place_values_kernel(put_ref, *refs):
    out_ref = refs[-1]
    most_rows = refs[0].shape[0]
    total = jnp.zeros(out_ref.shape, jnp.float32)
    for other, rows_ref in enumerate(refs[:-1]):
        total += jnp.dot(
            put_ref[other, :, :most_rows], rows_ref[...], preferred_element_type=jnp.float32
        )
    out_ref[...] = total.astype(jnp.bfloat16)


def place_values(put, came):
    vmem = pl.BlockSpec(memory_space=pltpu.VMEM)
    return pl.pallas_call(
        place_values_kernel,
        out_shape=jax.ShapeDtypeStruct((OWN_DEV, came[0].shape[1]), jnp.bfloat16),
        in_specs=[vmem] * (1 + len(came)),
        out_specs=vmem,
        compiler_params=pltpu.CompilerParams(vmem_limit_bytes=VMEM_BYTES),
        name="place_values",
    )(put, *came)


def local(
    tokens,
    norm_gain,
    key_weight,
    value_weight,
    key_bias,
    value_bias,
    block_counts,
    positions,
    dest_slots,
):
    axes = ("rep", "fsdp")
    devices = lax.axis_size(axes)
    most_rows = (HOT_BLOCKS + 1) * (BLOCK // devices)
    capacity = devices * most_rows
    rows, width = tokens.shape
    depth = key_weight.shape[0]
    shards = lax.axis_size("fsdp")

    def exchange(rows_by_owner):
        return lax.all_to_all(rows_by_owner, axes, split_axis=0, concat_axis=0, tiled=True)

    got = lax.ppermute(tokens, "tp", [(0, 1), (1, 0)])
    quarter = depth // 4
    relayed = (
        shards == 2
        and lax.axis_size("groups") == 2
        and lax.axis_size("rep") % 2 == 0
        and depth % 4 == 0
        and quarter % 128 == 0
    )
    swap = [(0, 1), (1, 0)]
    if relayed:
        key_own, value_own, key_last, value_last = cut_quarters(key_weight, value_weight)
        key_own = lax.ppermute(key_own, "fsdp", swap)
        value_own = lax.ppermute(value_own, "fsdp", swap)
        got, key_last, value_last = ordered(got, key_last, value_last)
        key_last = lax.ppermute(key_last, "fsdp", swap)
        value_last = lax.ppermute(value_last, "fsdp", swap)

    near_keys, near_values, scale = near_part(
        tokens,
        got,
        norm_gain,
        key_weight,
        value_weight,
        key_bias,
        value_bias,
    )
    if relayed:
        across = [(i, i ^ 1) for i in range(lax.axis_size("rep"))]
        key_own, near_values = ordered(key_own, near_values)

        def pieces_of(own, opposite):
            by_group = lax.ppermute(own, "groups", swap)
            by_rep = lax.ppermute(own, "rep", across)
            return own, by_group, by_rep, opposite

        key_pieces = pieces_of(key_own, key_last)
        value_pieces = pieces_of(value_own, value_last)
    else:
        steps = range(1, shards)

        def pieces_of(weight):
            return tuple(
                lax.ppermute(weight, "fsdp", [(i, (i + k) % shards) for i in range(shards)])
                for k in steps
            )

        key_pieces = pieces_of(key_weight)
        value_pieces = pieces_of(value_weight)

    columns = key_weight.shape[1]
    inline = most_rows % 16 == 0 and most_rows <= columns
    target, marks = route(block_counts, dest_slots, devices, most_rows, columns, near_values)
    positions, near_values = ordered(positions, near_values)
    angles = rotary_angles(positions)
    if not inline:
        got_marks = exchange(marks[:, 0, :most_rows].reshape(capacity))
    (send_keys,) = far_part(
        relayed,
        (tokens, got),
        norm_gain,
        near_keys,
        scale,
        key_pieces,
        angles,
        target,
        capacity,
        marks if inline else None,
        1,
        value_pieces[0],
    )
    came_keys = exchange(send_keys)
    paired = inline and devices & (devices - 1) == 0 and most_rows <= 128
    send_values = far_part(
        relayed,
        (tokens, got),
        norm_gain,
        near_values,
        scale,
        value_pieces,
        (),
        target,
        capacity,
        None,
        devices if paired else 1,
        send_keys,
    )
    if paired:
        came_values = list(send_values)
        for other in sorted(range(1, devices), key=lambda k: -(k ^ 2)):
            came_values[other] = lax.ppermute(
                send_values[other], axes, [(i, i ^ other) for i in range(devices)]
            )
        put, cache_keys = place_keys(came_keys)
        return cache_keys, place_values(put, came_values)
    came_values = exchange(send_values[0])
    if inline:
        got_marks = came_keys[:, most_rows, :most_rows].reshape(capacity)
        came_keys = came_keys[:, :most_rows].reshape(capacity, columns)
    put = (
        jnp.arange(OWN_DEV, dtype=jnp.int32)[:, None] == got_marks.astype(jnp.int32)[None, :]
    ).astype(jnp.bfloat16)
    return tuple(
        jnp.dot(put, came, preferred_element_type=jnp.float32).astype(jnp.bfloat16)
        for came in (came_keys, came_values)
    )


def solution(mesh):
    return jax.shard_map(
        local,
        mesh=mesh,
        in_specs=(
            P(("groups", "rep", "fsdp"), "tp"),
            P(),
            P("fsdp", "tp"),
            P("fsdp", "tp"),
            P("tp"),
            P("tp"),
            P("groups"),
            P(("groups", "rep", "fsdp")),
            P(("groups", "rep", "fsdp")),
        ),
        out_specs=(P(("groups", "rep", "fsdp"), "tp"), P(("groups", "rep", "fsdp"), "tp")),
        check_vma=False,
    )
```

```python
import functools

import jax
import jax.numpy as jnp
from jax import lax
from jax.experimental import pallas as pl
from jax.experimental.pallas import tpu as pltpu
from jax.sharding import PartitionSpec as P

HEAD_DIM = 128
BLOCK = 128
HOT_BLOCKS = 5
OWN_DEV = 256


epsilon = 1e-05
rope_base = 1000000.0
VMEM_BYTES = 62 * 1024 * 1024
VMEM_PLACE = 16 * 1024 * 1024
NEAR_STEP = 128
NEAR_AHEAD = 4
NEAR_COST = 20_000_000_000
FAR_COST = 20_000_000_000


def ordered(*values):
    return lax.optimization_barrier(values)


def group_index():
    return lax.axis_index("rep") * lax.axis_size("fsdp") + lax.axis_index("fsdp")


def quarter_numbers():
    group = lax.axis_index("groups")
    odd = lax.rem(lax.axis_index("rep"), 2)
    return (2 * group + odd, 2 * (1 - group) + odd, 2 * group + 1 - odd, 3 - 2 * group - odd)


def far_places(relayed, depth):
    shards = lax.axis_size("fsdp")
    shard = lax.axis_index("fsdp")
    if relayed:
        return [(1 - shard) * depth + number * (depth // 4) for number in quarter_numbers()]
    return [lax.rem(shard + shards - k, shards) * depth for k in range(1, shards)]


def rotary_angles(positions):
    half_rot = HEAD_DIM // 4
    freq_index = jnp.arange(half_rot, dtype=jnp.float32)
    inverse = rope_base ** (-freq_index / half_rot)
    angles = inverse[:, None] * positions.astype(jnp.float32)[None, :]
    return jnp.cos(angles), jnp.sin(angles)


def cut_kernel(opposite, *refs):
    count = len(opposite)
    sources, outs, sems = refs[:count], refs[count : 2 * count], refs[-1]
    quarter = outs[0].shape[0]
    mine, last = quarter_numbers()[0], quarter_numbers()[3]
    copies = []
    for index, source in enumerate(sources):
        start = pl.multiple_of((last if opposite[index] else mine) * quarter, quarter)
        copy = pltpu.make_async_copy(
            source.at[pl.ds(start, quarter), :], outs[index], sems.at[index]
        )
        copy.start()
        copies.append(copy)
    for copy in copies:
        copy.wait()


def cut_quarters(weights, opposite):
    count = len(weights)
    depth, columns = weights[0].shape
    piece = jax.ShapeDtypeStruct((depth // 4, columns), weights[0].dtype)
    return pl.pallas_call(
        functools.partial(cut_kernel, opposite),
        out_shape=(piece,) * count,
        in_specs=[pl.BlockSpec(memory_space=pl.ANY)] * count,
        out_specs=(pl.BlockSpec(memory_space=pltpu.VMEM),) * count,
        scratch_shapes=[pltpu.SemaphoreType.DMA((count,))],
        compiler_params=pltpu.CompilerParams(vmem_limit_bytes=VMEM_BYTES),
        name="cut_quarters",
    )(*weights)


def near_kernel(
    own_ref,
    got_ref,
    key_ref,
    value_ref,
    gain_ref,
    key_bias_ref,
    value_bias_ref,
    keys_ref,
    values_ref,
    scale_ref,
    own_buf,
    got_buf,
    key_buf,
    value_buf,
    normed_ref,
    key_sum,
    value_sum,
    scale_buf,
    sems,
):
    rows, width = own_ref.shape
    depth = key_ref.shape[0]
    size = NEAR_STEP
    blocks = rows // size

    def read(index):
        if index == blocks:
            pairs = ((key_ref, key_buf), (value_ref, value_buf))
        else:
            here = pl.ds(index * size, size)
            pairs = (
                (own_ref.at[here, :], own_buf.at[here, :]),
                (got_ref.at[here, :], got_buf.at[here, :]),
            )
        return [
            pltpu.make_async_copy(source, buf, sems.at[side, index])
            for side, (source, buf) in enumerate(pairs)
        ]

    def start(index):
        if index <= blocks:
            for copy in read(index):
                copy.start()

    for index in range(NEAR_AHEAD):
        start(index)
    lanes = 128
    near_first = lax.axis_index("fsdp") * depth
    side = near_first // width
    gain = gain_ref[pl.ds(pl.multiple_of(side * width, width), width)]
    gain = gain.astype(jnp.float32).reshape(1, width)
    writes = []
    for index in range(blocks):
        for copy in read(index):
            copy.wait()
        start(index + NEAR_AHEAD)
        here = pl.ds(index * size, size)
        squares = jnp.zeros((size, lanes), jnp.float32)
        for source in (own_buf, got_buf):
            for first in range(0, width, lanes):
                part = source[here, first : first + lanes].astype(jnp.float32)
                squares += part * part
        total = jnp.sum(squares, axis=1, keepdims=True)
        scale = jnp.broadcast_to(lax.rsqrt(total / (2 * width) + epsilon), (size, lanes))
        scale_buf[here, :] = scale
        for source, is_near in (
            (own_buf, side == lax.axis_index("tp")),
            (got_buf, side != lax.axis_index("tp")),
        ):

            @pl.when(is_near)
            def _(source=source, here=here, scale=scale):
                for first in range(0, width, lanes):
                    part = source[here, first : first + lanes].astype(jnp.float32)
                    normed_ref[here, first : first + lanes] = (
                        part * scale * gain[:, first : first + lanes]
                    ).astype(jnp.bfloat16)

    write = pltpu.make_async_copy(scale_buf, scale_ref, sems.at[2, 0])
    write.start()
    writes.append(write)
    for copy in read(blocks):
        copy.wait()
    for weight, bias_ref, sum_ref, out_ref in (
        (key_buf, key_bias_ref, key_sum, keys_ref),
        (value_buf, value_bias_ref, value_sum, values_ref),
    ):
        bias = bias_ref[...].astype(jnp.float32).reshape(1, sum_ref.shape[1])
        near = normed_ref[:, pl.ds(pl.multiple_of(near_first % width, depth), depth)]
        sum_ref[...] = jnp.dot(near, weight[...], preferred_element_type=jnp.float32) + bias
        write = pltpu.make_async_copy(sum_ref, out_ref, sems.at[2, len(writes)])
        write.start()
        writes.append(write)
    for write in writes:
        write.wait()


def near_part(own, got, norm_gain, key_weight, value_weight, key_bias, value_bias):
    rows, width = own.shape
    depth, columns = key_weight.shape
    sums = jax.ShapeDtypeStruct((rows, columns), jnp.float32)
    vmem = pl.BlockSpec(memory_space=pltpu.VMEM)
    anywhere = pl.BlockSpec(memory_space=pl.ANY)
    return pl.pallas_call(
        near_kernel,
        out_shape=(sums, sums, jax.ShapeDtypeStruct((rows, 128), jnp.float32)),
        in_specs=[anywhere] * 4 + [vmem] * 3,
        out_specs=(anywhere,) * 3,
        scratch_shapes=[
            pltpu.VMEM((rows, width), jnp.bfloat16),
            pltpu.VMEM((rows, width), jnp.bfloat16),
            pltpu.VMEM((depth, columns), jnp.bfloat16),
            pltpu.VMEM((depth, columns), jnp.bfloat16),
            pltpu.VMEM((rows, width), jnp.bfloat16),
            pltpu.VMEM((rows, columns), jnp.float32),
            pltpu.VMEM((rows, columns), jnp.float32),
            pltpu.VMEM((rows, 128), jnp.float32),
            pltpu.SemaphoreType.DMA((3, rows // NEAR_STEP + 1)),
        ],
        compiler_params=pltpu.CompilerParams(vmem_limit_bytes=VMEM_BYTES),
        cost_estimate=pl.CostEstimate(
            flops=NEAR_COST,
            bytes_accessed=6 * rows * width + 4 * depth * columns,
            transcendentals=0,
        ),
        name="near_part",
    )(own, got, key_weight, value_weight, norm_gain, key_bias, value_bias)


def turned(total, cosine, sine):
    half_rot, rows = cosine.shape
    rest = jnp.zeros((HEAD_DIM - 2 * half_rot, rows), jnp.float32)
    straight = jnp.concatenate([cosine, cosine, rest + 1.0], axis=0).T
    crossed = jnp.concatenate([-sine, sine, rest], axis=0).T
    lane = lax.broadcasted_iota(jnp.int32, straight.shape, 1)
    heads = []
    for head in range(total.shape[1] // HEAD_DIM):
        part = total[:, head * HEAD_DIM : (head + 1) * HEAD_DIM]
        partner = jnp.where(
            lane < half_rot,
            pltpu.roll(part, HEAD_DIM - half_rot, 1),
            pltpu.roll(part, half_rot, 1),
        )
        heads.append(part * straight + partner * crossed)
    return jnp.concatenate(heads, axis=1)


def picked(target_ref, first, size, rows):
    target = target_ref[0:1, :]
    line = lax.broadcasted_iota(jnp.int32, (size, target.shape[1]), 0) + first
    pick = jnp.where(line == target, 1.0, 0.0).astype(jnp.bfloat16)
    return jnp.dot(pick, rows, preferred_element_type=jnp.float32).astype(jnp.bfloat16)


def far_kernel(relayed, turn, extra, count, outs, *refs):
    own_ref, got_ref, near_ref, scale_ref = refs[:4]
    pieces = refs[4 : 4 + count]
    scratch = refs[-2 * count - 5 :]
    part_bufs, piece_bufs = scratch[:count], scratch[count : 2 * count]
    near_buf, scale_buf, gain_buf, normed_buf, sems = scratch[2 * count :]
    rest = list(refs[4 + count : -outs - 1 - len(scratch)])
    out_refs = refs[-outs - len(scratch) : -len(scratch)]
    depth = pieces[0].shape[0]
    width = own_ref.shape[1]
    places = far_places(relayed, depth * 4 if relayed else depth)
    lanes = 128
    near_copies = (
        pltpu.make_async_copy(near_ref, near_buf, sems.at[0, count]),
        pltpu.make_async_copy(scale_ref, scale_buf, sems.at[1, count]),
    )

    def part_copy(source, index):
        first = pl.multiple_of(places[index] % width, lanes)
        return pltpu.make_async_copy(
            source.at[:, pl.ds(first, depth)], part_bufs[index], sems.at[0, index]
        )

    def piece_copy(index):
        return pltpu.make_async_copy(pieces[index], piece_bufs[index], sems.at[1, index])

    for copy in near_copies:
        copy.start()
    for index in range(count):
        is_own = places[index] // width == lax.axis_index("tp")

        @pl.when(is_own)
        def _(index=index):
            part_copy(own_ref, index).start()

        @pl.when(jnp.logical_not(is_own))
        def _(index=index):
            part_copy(got_ref, index).start()

        piece_copy(index).start()
    gain_ref = rest.pop(0)
    gain_buf[...] = gain_ref[...].astype(jnp.float32).reshape(1, 2 * width)
    for copy in near_copies:
        copy.wait()
    total = near_buf[...]
    for index in range(count):
        part_copy(own_ref, index).wait()
        for first in range(0, depth, lanes):
            here = slice(first, first + lanes)
            gain = gain_buf[:, pl.ds(pl.multiple_of(places[index] + first, lanes), lanes)]
            part = part_bufs[index][:, here].astype(jnp.float32)
            normed_buf[:, here] = (part * scale_buf[...] * gain).astype(jnp.bfloat16)
        piece_copy(index).wait()
        total += jnp.dot(
            normed_buf[...], piece_bufs[index][...], preferred_element_type=jnp.float32
        )
    if turn:
        total = turned(total, rest.pop(0)[...], rest.pop(0)[...])
    target_ref = rest.pop(0)
    total = total.astype(jnp.bfloat16)
    if outs > 1:
        me = group_index()
        for other, out_ref in enumerate(out_refs):
            size = out_ref.shape[0]
            out_ref[...] = picked(target_ref, lax.bitwise_xor(me, other) * size, size, total)
    elif extra:
        extra_ref = rest.pop(0)
        owners, tall, columns = out_refs[0].shape
        most_rows = tall - extra
        laid = picked(target_ref, 0, owners * most_rows, total)
        out_refs[0][:, :most_rows, :] = laid.reshape(owners, most_rows, columns)
        out_refs[0][:, most_rows:, :] = extra_ref[...]
    else:
        out_refs[0][...] = picked(target_ref, 0, out_refs[0].shape[0], total)


def far_part(
    relayed, rows_of, norm_gain, near, scale, pieces, angles, target, capacity, extra, outs, after
):
    rows, columns = near.shape
    depth = pieces[0].shape[0]
    count = len(pieces)
    operands = [norm_gain, *angles, target]
    tall = 0
    if extra is None:
        shape = (capacity // outs, columns)
    else:
        owners, tall, _ = extra.shape
        shape = (owners, capacity // owners + tall, columns)
        operands.append(extra)
    vmem = pl.BlockSpec(memory_space=pltpu.VMEM)
    anywhere = pl.BlockSpec(memory_space=pl.ANY)
    return pl.pallas_call(
        functools.partial(far_kernel, relayed, bool(angles), tall, count, outs),
        out_shape=(jax.ShapeDtypeStruct(shape, jnp.bfloat16),) * outs,
        in_specs=[anywhere] * (4 + count) + [vmem] * len(operands) + [anywhere],
        out_specs=(vmem,) * outs,
        scratch_shapes=[
            *[pltpu.VMEM((rows, depth), jnp.bfloat16) for _ in pieces],
            *[pltpu.VMEM((depth, columns), jnp.bfloat16) for _ in pieces],
            pltpu.VMEM((rows, columns), jnp.float32),
            pltpu.VMEM(scale.shape, jnp.float32),
            pltpu.VMEM((1, norm_gain.shape[0]), jnp.float32),
            pltpu.VMEM((rows, depth), jnp.bfloat16),
            pltpu.SemaphoreType.DMA((2, count + 1)),
        ],
        compiler_params=pltpu.CompilerParams(vmem_limit_bytes=VMEM_BYTES),
        cost_estimate=pl.CostEstimate(
            flops=FAR_COST,
            bytes_accessed=12 * rows * columns,
            transcendentals=0,
        ),
        name="far_part",
    )(*rows_of, near, scale, *pieces, *operands, after)


def route_kernel(most_rows, counts_ref, dest_ref, after_ref, target_ref, marks_ref):
    me = group_index()
    devices = marks_ref.shape[0]
    rows = dest_ref.shape[0]
    dest = dest_ref[...].reshape(1, rows)
    row = lax.broadcasted_iota(jnp.int32, (1, rows), 1)
    valid = (row < BLOCK * counts_ref[me]) & (dest >= 0)
    owner = jnp.where(valid, lax.div(dest, OWN_DEV), -1)
    slot = jnp.where(valid, lax.rem(dest, OWN_DEV), -1)
    tall = -(-devices // 16) * 16
    to_owner = lax.broadcasted_iota(jnp.int32, (tall, rows), 0) == owner
    ones = jnp.where(to_owner, 1.0, 0.0)
    earlier = jnp.where(
        lax.broadcasted_iota(jnp.int32, (rows, rows), 0)
        < lax.broadcasted_iota(jnp.int32, (rows, rows), 1),
        1.0,
        0.0,
    ).astype(jnp.bfloat16)
    before = jnp.dot(ones.astype(jnp.bfloat16), earlier, preferred_element_type=jnp.float32)
    rank = jnp.sum(ones * before, axis=0, keepdims=True).astype(jnp.int32)
    target = jnp.where(valid, owner * most_rows + rank, devices * most_rows)
    target_ref[...] = jnp.broadcast_to(target, target_ref.shape)
    at_rank = jnp.where(
        (lax.broadcasted_iota(jnp.int32, (marks_ref.shape[2], rows), 0) == rank) & valid, 1.0, 0.0
    ).astype(jnp.bfloat16)
    slots = jnp.where(to_owner, (slot + 1).astype(jnp.float32), 0.0).astype(jnp.bfloat16)
    marks = lax.dot_general(
        slots, at_rank, (((1,), (1,)), ((), ())), preferred_element_type=jnp.float32
    )
    marks = marks[:devices] - 1.0
    marks_ref[...] = jnp.broadcast_to(marks[:, None, :], marks_ref.shape).astype(jnp.bfloat16)


def route(block_counts, dest_slots, devices, most_rows, columns, after):
    rows = dest_slots.shape[0]
    vmem = pl.BlockSpec(memory_space=pltpu.VMEM)
    return pl.pallas_call(
        functools.partial(route_kernel, most_rows),
        out_shape=(
            jax.ShapeDtypeStruct((8, rows), jnp.int32),
            jax.ShapeDtypeStruct((devices, 16, columns), jnp.bfloat16),
        ),
        in_specs=[
            pl.BlockSpec(memory_space=pltpu.SMEM),
            vmem,
            pl.BlockSpec(memory_space=pl.ANY),
        ],
        out_specs=(vmem,) * 2,
        compiler_params=pltpu.CompilerParams(vmem_limit_bytes=VMEM_BYTES),
        name="route",
    )(block_counts, dest_slots, after)


def put_rows(slots, rows_ref, owned):
    slot = lax.broadcasted_iota(jnp.int32, (owned, slots.shape[1]), 0)
    put = jnp.where(slot == slots, 1.0, 0.0).astype(jnp.bfloat16)
    return jnp.dot(put, rows_ref[: slots.shape[1], :], preferred_element_type=jnp.float32)


def place_kernel(came_ref, values_ref, slots_ref, started_ref, out_ref):
    devices, tall, columns = came_ref.shape
    most_rows = tall - 16
    owned = out_ref.shape[0]
    total = jnp.zeros(out_ref.shape, jnp.float32)
    me = group_index()
    for other in range(devices):
        source = lax.bitwise_xor(me, other)
        marks = came_ref[source, most_rows:, :].astype(jnp.float32)[0:8].astype(jnp.int32)
        slots_ref[other] = marks[:, :128]
        total += put_rows(marks[0:1, :most_rows], came_ref.at[source], owned)
        if other == 0:
            started_ref[...] = put_rows(marks[0:1, :most_rows], values_ref, owned)
    out_ref[...] = total.astype(jnp.bfloat16)


def place_keys(came, own_values):
    devices, tall, columns = came.shape
    vmem = pl.BlockSpec(memory_space=pltpu.VMEM)
    return pl.pallas_call(
        place_kernel,
        out_shape=(
            jax.ShapeDtypeStruct((devices, 8, 128), jnp.int32),
            jax.ShapeDtypeStruct((OWN_DEV, columns), jnp.float32),
            jax.ShapeDtypeStruct((OWN_DEV, columns), jnp.bfloat16),
        ),
        in_specs=[vmem] * 2,
        out_specs=(vmem,) * 3,
        compiler_params=pltpu.CompilerParams(vmem_limit_bytes=VMEM_PLACE),
        name="place_keys",
    )(came, own_values)


def place_values_kernel(slots_ref, started_ref, *refs):
    out_ref = refs[-1]
    total = started_ref[...]
    for other, rows_ref in enumerate(refs[:-1]):
        slots = slots_ref[other + 1, 0:1, : rows_ref.shape[0]]
        total += put_rows(slots, rows_ref, out_ref.shape[0])
    out_ref[...] = total.astype(jnp.bfloat16)


def place_values(slots, started, came):
    vmem = pl.BlockSpec(memory_space=pltpu.VMEM)
    return pl.pallas_call(
        place_values_kernel,
        out_shape=jax.ShapeDtypeStruct(started.shape, jnp.bfloat16),
        in_specs=[vmem] * (2 + len(came)),
        out_specs=vmem,
        compiler_params=pltpu.CompilerParams(vmem_limit_bytes=VMEM_PLACE),
        name="place_values",
    )(slots, started, *came)


def local(
    tokens,
    norm_gain,
    key_weight,
    value_weight,
    key_bias,
    value_bias,
    block_counts,
    positions,
    dest_slots,
):
    axes = ("rep", "fsdp")
    devices = lax.axis_size(axes)
    most_rows = (HOT_BLOCKS + 1) * (BLOCK // devices)
    capacity = devices * most_rows
    rows, width = tokens.shape
    depth = key_weight.shape[0]
    shards = lax.axis_size("fsdp")

    def exchange(rows_by_owner):
        return lax.all_to_all(rows_by_owner, axes, split_axis=0, concat_axis=0, tiled=True)

    got = lax.ppermute(tokens, "tp", [(0, 1), (1, 0)])
    quarter = depth // 4
    relayed = (
        shards == 2
        and lax.axis_size("groups") == 2
        and lax.axis_size("rep") % 2 == 0
        and depth % 4 == 0
        and quarter % 128 == 0
    )
    swap = [(0, 1), (1, 0)]
    if relayed:
        (key_own,) = cut_quarters((key_weight,), (False,))
        value_own, key_last, value_last = cut_quarters(
            (value_weight, key_weight, value_weight), (False, True, True)
        )
        key_own = lax.ppermute(key_own, "fsdp", swap)
        value_own = lax.ppermute(value_own, "fsdp", swap)
        got, key_last, value_last = ordered(got, key_last, value_last)
        key_last = lax.ppermute(key_last, "fsdp", swap)
        value_last = lax.ppermute(value_last, "fsdp", swap)

    near_keys, near_values, scale = near_part(
        tokens,
        got,
        norm_gain,
        key_weight,
        value_weight,
        key_bias,
        value_bias,
    )
    if relayed:
        across = [(i, i ^ 1) for i in range(lax.axis_size("rep"))]
        key_own, near_values = ordered(key_own, near_values)

        def pieces_of(own, opposite):
            by_group = lax.ppermute(own, "groups", swap)
            by_rep = lax.ppermute(own, "rep", across)
            return own, by_group, by_rep, opposite

        key_pieces = pieces_of(key_own, key_last)
        value_pieces = pieces_of(value_own, value_last)
    else:
        steps = range(1, shards)

        def pieces_of(weight):
            return tuple(
                lax.ppermute(weight, "fsdp", [(i, (i + k) % shards) for i in range(shards)])
                for k in steps
            )

        key_pieces = pieces_of(key_weight)
        value_pieces = pieces_of(value_weight)

    columns = key_weight.shape[1]
    inline = most_rows % 16 == 0 and most_rows <= columns
    target, marks = route(block_counts, dest_slots, devices, most_rows, columns, near_values)
    positions, near_values = ordered(positions, near_values)
    angles = rotary_angles(positions)
    if not inline:
        got_marks = exchange(marks[:, 0, :most_rows].reshape(capacity))
    (send_keys,) = far_part(
        relayed,
        (tokens, got),
        norm_gain,
        near_keys,
        scale,
        key_pieces,
        angles,
        target,
        capacity,
        marks if inline else None,
        1,
        value_pieces[0],
    )
    came_keys = exchange(send_keys)
    paired = inline and devices & (devices - 1) == 0 and most_rows <= 128
    send_values = far_part(
        relayed,
        (tokens, got),
        norm_gain,
        near_values,
        scale,
        value_pieces,
        (),
        target,
        capacity,
        None,
        devices if paired else 1,
        send_keys,
    )
    if paired:
        came_values = list(send_values)
        for other in sorted(range(1, devices), key=lambda k: -(k ^ 2)):
            came_values[other] = lax.ppermute(
                send_values[other], axes, [(i, i ^ other) for i in range(devices)]
            )
        slots, started, cache_keys = place_keys(came_keys, send_values[0])
        return cache_keys, place_values(slots, started, came_values[1:])
    came_values = exchange(send_values[0])
    if inline:
        got_marks = came_keys[:, most_rows, :most_rows].reshape(capacity)
        came_keys = came_keys[:, :most_rows].reshape(capacity, columns)
    put = (
        jnp.arange(OWN_DEV, dtype=jnp.int32)[:, None] == got_marks.astype(jnp.int32)[None, :]
    ).astype(jnp.bfloat16)
    return tuple(
        jnp.dot(put, came, preferred_element_type=jnp.float32).astype(jnp.bfloat16)
        for came in (came_keys, came_values)
    )


def solution(mesh):
    return jax.shard_map(
        local,
        mesh=mesh,
        in_specs=(
            P(("groups", "rep", "fsdp"), "tp"),
            P(),
            P("fsdp", "tp"),
            P("fsdp", "tp"),
            P("tp"),
            P("tp"),
            P("groups"),
            P(("groups", "rep", "fsdp")),
            P(("groups", "rep", "fsdp")),
        ),
        out_specs=(P(("groups", "rep", "fsdp"), "tp"), P(("groups", "rep", "fsdp"), "tp")),
        check_vma=False,
    )
```

```python
import functools

import jax
import jax.numpy as jnp
from jax import lax
from jax.experimental import pallas as pl
from jax.experimental.pallas import tpu as pltpu
from jax.sharding import PartitionSpec as P

HEAD_DIM = 128
BLOCK = 128
HOT_BLOCKS = 5
OWN_DEV = 256


epsilon = 1e-05
rope_base = 1000000.0
VMEM_BYTES = 63 * 1024 * 1024
VMEM_PLACE = 16 * 1024 * 1024
NEAR_STEP = 128
NEAR_AHEAD = 4
NEAR_COST = 20_000_000_000
FAR_COST = 20_000_000_000


def ordered(*values):
    return lax.optimization_barrier(values)


def group_index():
    return lax.axis_index("rep") * lax.axis_size("fsdp") + lax.axis_index("fsdp")


def quarter_numbers():
    group = lax.axis_index("groups")
    odd = lax.rem(lax.axis_index("rep"), 2)
    return (2 * group + odd, 2 * (1 - group) + odd, 2 * group + 1 - odd, 3 - 2 * group - odd)


def far_places(relayed, depth):
    shards = lax.axis_size("fsdp")
    shard = lax.axis_index("fsdp")
    if relayed:
        return [(1 - shard) * depth + number * (depth // 4) for number in quarter_numbers()]
    return [lax.rem(shard + shards - k, shards) * depth for k in range(1, shards)]


def rotary_angles(positions):
    half_rot = HEAD_DIM // 4
    freq_index = jnp.arange(half_rot, dtype=jnp.float32)
    inverse = rope_base ** (-freq_index / half_rot)
    angles = inverse[:, None] * positions.astype(jnp.float32)[None, :]
    return jnp.cos(angles), jnp.sin(angles)


def cut_kernel(opposite, *refs):
    count = len(opposite)
    sources, outs, sems = refs[:count], refs[count : 2 * count], refs[-1]
    quarter = outs[0].shape[0]
    mine, last = quarter_numbers()[0], quarter_numbers()[3]
    copies = []
    for index, source in enumerate(sources):
        start = pl.multiple_of((last if opposite[index] else mine) * quarter, quarter)
        copy = pltpu.make_async_copy(
            source.at[pl.ds(start, quarter), :], outs[index], sems.at[index]
        )
        copy.start()
        copies.append(copy)
    for copy in copies:
        copy.wait()


def cut_quarters(weights, opposite):
    count = len(weights)
    depth, columns = weights[0].shape
    piece = jax.ShapeDtypeStruct((depth // 4, columns), weights[0].dtype)
    return pl.pallas_call(
        functools.partial(cut_kernel, opposite),
        out_shape=(piece,) * count,
        in_specs=[pl.BlockSpec(memory_space=pl.ANY)] * count,
        out_specs=(pl.BlockSpec(memory_space=pltpu.VMEM),) * count,
        scratch_shapes=[pltpu.SemaphoreType.DMA((count,))],
        compiler_params=pltpu.CompilerParams(vmem_limit_bytes=VMEM_BYTES),
        name="cut_quarters",
    )(*weights)


def near_kernel(
    own_ref,
    got_ref,
    key_ref,
    value_ref,
    gain_ref,
    key_bias_ref,
    value_bias_ref,
    keys_ref,
    values_ref,
    scale_ref,
    own_buf,
    got_buf,
    key_buf,
    value_buf,
    normed_ref,
    key_sum,
    value_sum,
    scale_buf,
    sems,
):
    rows, width = own_ref.shape
    depth = key_ref.shape[0]
    size = NEAR_STEP
    blocks = rows // size

    def read(index):
        if index == blocks:
            pairs = ((key_ref, key_buf), (value_ref, value_buf))
        else:
            here = pl.ds(index * size, size)
            pairs = (
                (own_ref.at[here, :], own_buf.at[here, :]),
                (got_ref.at[here, :], got_buf.at[here, :]),
            )
        return [
            pltpu.make_async_copy(source, buf, sems.at[side, index])
            for side, (source, buf) in enumerate(pairs)
        ]

    def start(index):
        if index <= blocks:
            for copy in read(index):
                copy.start()

    for index in range(NEAR_AHEAD):
        start(index)
    lanes = 128
    near_first = lax.axis_index("fsdp") * depth
    side = near_first // width
    gain = gain_ref[pl.ds(pl.multiple_of(side * width, width), width)]
    gain = gain.astype(jnp.float32).reshape(1, width)
    writes = []
    for index in range(blocks):
        for copy in read(index):
            copy.wait()
        start(index + NEAR_AHEAD)
        here = pl.ds(index * size, size)
        squares = jnp.zeros((size, lanes), jnp.float32)
        for source in (own_buf, got_buf):
            for first in range(0, width, lanes):
                part = source[here, first : first + lanes].astype(jnp.float32)
                squares += part * part
        total = jnp.sum(squares, axis=1, keepdims=True)
        scale = jnp.broadcast_to(lax.rsqrt(total / (2 * width) + epsilon), (size, lanes))
        scale_buf[here, :] = scale
        for source, is_near in (
            (own_buf, side == lax.axis_index("tp")),
            (got_buf, side != lax.axis_index("tp")),
        ):

            @pl.when(is_near)
            def _(source=source, here=here, scale=scale):
                for first in range(0, width, lanes):
                    part = source[here, first : first + lanes].astype(jnp.float32)
                    normed_ref[here, first : first + lanes] = (
                        part * scale * gain[:, first : first + lanes]
                    ).astype(jnp.bfloat16)

    write = pltpu.make_async_copy(scale_buf, scale_ref, sems.at[2, 0])
    write.start()
    writes.append(write)
    for copy in read(blocks):
        copy.wait()
    for weight, bias_ref, sum_ref, out_ref in (
        (key_buf, key_bias_ref, key_sum, keys_ref),
        (value_buf, value_bias_ref, value_sum, values_ref),
    ):
        bias = bias_ref[...].astype(jnp.float32).reshape(1, sum_ref.shape[1])
        near = normed_ref[:, pl.ds(pl.multiple_of(near_first % width, depth), depth)]
        sum_ref[...] = jnp.dot(near, weight[...], preferred_element_type=jnp.float32) + bias
        write = pltpu.make_async_copy(sum_ref, out_ref, sems.at[2, len(writes)])
        write.start()
        writes.append(write)
    for write in writes:
        write.wait()


def near_part(own, got, norm_gain, key_weight, value_weight, key_bias, value_bias):
    rows, width = own.shape
    depth, columns = key_weight.shape
    sums = jax.ShapeDtypeStruct((rows, columns), jnp.float32)
    vmem = pl.BlockSpec(memory_space=pltpu.VMEM)
    anywhere = pl.BlockSpec(memory_space=pl.ANY)
    return pl.pallas_call(
        near_kernel,
        out_shape=(sums, sums, jax.ShapeDtypeStruct((rows, 128), jnp.float32)),
        in_specs=[anywhere] * 4 + [vmem] * 3,
        out_specs=(anywhere,) * 3,
        scratch_shapes=[
            pltpu.VMEM((rows, width), jnp.bfloat16),
            pltpu.VMEM((rows, width), jnp.bfloat16),
            pltpu.VMEM((depth, columns), jnp.bfloat16),
            pltpu.VMEM((depth, columns), jnp.bfloat16),
            pltpu.VMEM((rows, width), jnp.bfloat16),
            pltpu.VMEM((rows, columns), jnp.float32),
            pltpu.VMEM((rows, columns), jnp.float32),
            pltpu.VMEM((rows, 128), jnp.float32),
            pltpu.SemaphoreType.DMA((3, rows // NEAR_STEP + 1)),
        ],
        compiler_params=pltpu.CompilerParams(vmem_limit_bytes=VMEM_BYTES),
        cost_estimate=pl.CostEstimate(
            flops=NEAR_COST,
            bytes_accessed=6 * rows * width + 4 * depth * columns,
            transcendentals=0,
        ),
        name="near_part",
    )(own, got, key_weight, value_weight, norm_gain, key_bias, value_bias)


def turned(total, cosine, sine):
    half_rot, rows = cosine.shape
    rest = jnp.zeros((HEAD_DIM - 2 * half_rot, rows), jnp.float32)
    straight = jnp.concatenate([cosine, cosine, rest + 1.0], axis=0).T
    crossed = jnp.concatenate([-sine, sine, rest], axis=0).T
    lane = lax.broadcasted_iota(jnp.int32, straight.shape, 1)
    heads = []
    for head in range(total.shape[1] // HEAD_DIM):
        part = total[:, head * HEAD_DIM : (head + 1) * HEAD_DIM]
        partner = jnp.where(
            lane < half_rot,
            pltpu.roll(part, HEAD_DIM - half_rot, 1),
            pltpu.roll(part, half_rot, 1),
        )
        heads.append(part * straight + partner * crossed)
    return jnp.concatenate(heads, axis=1)


def picked(target_ref, first, size, rows):
    target = target_ref[0:1, :]
    line = lax.broadcasted_iota(jnp.int32, (size, target.shape[1]), 0) + first
    pick = jnp.where(line == target, 1.0, 0.0).astype(jnp.bfloat16)
    return jnp.dot(pick, rows, preferred_element_type=jnp.float32).astype(jnp.bfloat16)


def far_kernel(relayed, turn, extra, count, outs, *refs):
    own_ref, got_ref, near_ref, scale_ref = refs[:4]
    pieces = refs[4 : 4 + count]
    scratch = refs[-2 * count - 5 :]
    part_bufs, piece_bufs = scratch[:count], scratch[count : 2 * count]
    near_buf, scale_buf, gain_buf, normed_buf, sems = scratch[2 * count :]
    rest = list(refs[4 + count : -outs - 1 - len(scratch)])
    out_refs = refs[-outs - len(scratch) : -len(scratch)]
    depth = pieces[0].shape[0]
    width = own_ref.shape[1]
    places = far_places(relayed, depth * 4 if relayed else depth)
    lanes = 128
    near_copies = (
        pltpu.make_async_copy(near_ref, near_buf, sems.at[0, count]),
        pltpu.make_async_copy(scale_ref, scale_buf, sems.at[1, count]),
    )

    def part_copy(source, index):
        first = pl.multiple_of(places[index] % width, lanes)
        return pltpu.make_async_copy(
            source.at[:, pl.ds(first, depth)], part_bufs[index], sems.at[0, index]
        )

    def piece_copy(index):
        return pltpu.make_async_copy(pieces[index], piece_bufs[index], sems.at[1, index])

    for copy in near_copies:
        copy.start()
    for index in range(count):
        is_own = places[index] // width == lax.axis_index("tp")

        @pl.when(is_own)
        def _(index=index):
            part_copy(own_ref, index).start()

        @pl.when(jnp.logical_not(is_own))
        def _(index=index):
            part_copy(got_ref, index).start()

        piece_copy(index).start()
    gain_ref = rest.pop(0)
    gain_buf[...] = gain_ref[...].astype(jnp.float32).reshape(1, 2 * width)
    for copy in near_copies:
        copy.wait()
    total = near_buf[...]
    for index in range(count):
        part_copy(own_ref, index).wait()
        for first in range(0, depth, lanes):
            here = slice(first, first + lanes)
            gain = gain_buf[:, pl.ds(pl.multiple_of(places[index] + first, lanes), lanes)]
            part = part_bufs[index][:, here].astype(jnp.float32)
            normed_buf[:, here] = (part * scale_buf[...] * gain).astype(jnp.bfloat16)
        piece_copy(index).wait()
        total += jnp.dot(
            normed_buf[...], piece_bufs[index][...], preferred_element_type=jnp.float32
        )
    if turn:
        total = turned(total, rest.pop(0)[...], rest.pop(0)[...])
    target_ref = rest.pop(0)
    total = total.astype(jnp.bfloat16)
    if outs > 1:
        me = group_index()
        for other, out_ref in enumerate(out_refs):
            size = out_ref.shape[0]
            out_ref[...] = picked(target_ref, lax.bitwise_xor(me, other) * size, size, total)
    elif extra:
        extra_ref = rest.pop(0)
        owners, tall, columns = out_refs[0].shape
        most_rows = tall - extra
        laid = picked(target_ref, 0, owners * most_rows, total)
        out_refs[0][:, :most_rows, :] = laid.reshape(owners, most_rows, columns)
        out_refs[0][:, most_rows:, :] = extra_ref[...]
    else:
        out_refs[0][...] = picked(target_ref, 0, out_refs[0].shape[0], total)


def far_part(
    relayed, rows_of, norm_gain, near, scale, pieces, angles, target, capacity, extra, outs, after
):
    rows, columns = near.shape
    depth = pieces[0].shape[0]
    count = len(pieces)
    operands = [norm_gain, *angles, target]
    tall = 0
    if extra is None:
        shape = (capacity // outs, columns)
    else:
        owners, tall, _ = extra.shape
        shape = (owners, capacity // owners + tall, columns)
        operands.append(extra)
    vmem = pl.BlockSpec(memory_space=pltpu.VMEM)
    anywhere = pl.BlockSpec(memory_space=pl.ANY)
    return pl.pallas_call(
        functools.partial(far_kernel, relayed, bool(angles), tall, count, outs),
        out_shape=(jax.ShapeDtypeStruct(shape, jnp.bfloat16),) * outs,
        in_specs=[anywhere] * (4 + count) + [vmem] * len(operands) + [anywhere],
        out_specs=(vmem,) * outs,
        scratch_shapes=[
            *[pltpu.VMEM((rows, depth), jnp.bfloat16) for _ in pieces],
            *[pltpu.VMEM((depth, columns), jnp.bfloat16) for _ in pieces],
            pltpu.VMEM((rows, columns), jnp.float32),
            pltpu.VMEM(scale.shape, jnp.float32),
            pltpu.VMEM((1, norm_gain.shape[0]), jnp.float32),
            pltpu.VMEM((rows, depth), jnp.bfloat16),
            pltpu.SemaphoreType.DMA((2, count + 1)),
        ],
        compiler_params=pltpu.CompilerParams(vmem_limit_bytes=VMEM_BYTES),
        cost_estimate=pl.CostEstimate(
            flops=FAR_COST,
            bytes_accessed=12 * rows * columns,
            transcendentals=0,
        ),
        name="far_part",
    )(*rows_of, near, scale, *pieces, *operands, after)


def route_kernel(most_rows, counts_ref, dest_ref, after_ref, target_ref, marks_ref):
    me = group_index()
    devices = marks_ref.shape[0]
    rows = dest_ref.shape[0]
    dest = dest_ref[...].reshape(1, rows)
    row = lax.broadcasted_iota(jnp.int32, (1, rows), 1)
    valid = (row < BLOCK * counts_ref[me]) & (dest >= 0)
    owner = jnp.where(valid, lax.div(dest, OWN_DEV), -1)
    slot = jnp.where(valid, lax.rem(dest, OWN_DEV), -1)
    tall = -(-devices // 16) * 16
    to_owner = lax.broadcasted_iota(jnp.int32, (tall, rows), 0) == owner
    ones = jnp.where(to_owner, 1.0, 0.0)
    earlier = jnp.where(
        lax.broadcasted_iota(jnp.int32, (rows, rows), 0)
        < lax.broadcasted_iota(jnp.int32, (rows, rows), 1),
        1.0,
        0.0,
    ).astype(jnp.bfloat16)
    before = jnp.dot(ones.astype(jnp.bfloat16), earlier, preferred_element_type=jnp.float32)
    rank = jnp.sum(ones * before, axis=0, keepdims=True).astype(jnp.int32)
    target = jnp.where(valid, owner * most_rows + rank, devices * most_rows)
    target_ref[...] = jnp.broadcast_to(target, target_ref.shape)
    at_rank = jnp.where(
        (lax.broadcasted_iota(jnp.int32, (marks_ref.shape[2], rows), 0) == rank) & valid, 1.0, 0.0
    ).astype(jnp.bfloat16)
    slots = jnp.where(to_owner, (slot + 1).astype(jnp.float32), 0.0).astype(jnp.bfloat16)
    marks = lax.dot_general(
        slots, at_rank, (((1,), (1,)), ((), ())), preferred_element_type=jnp.float32
    )
    marks = marks[:devices] - 1.0
    marks_ref[...] = jnp.broadcast_to(marks[:, None, :], marks_ref.shape).astype(jnp.bfloat16)


def route(block_counts, dest_slots, devices, most_rows, columns, after):
    rows = dest_slots.shape[0]
    vmem = pl.BlockSpec(memory_space=pltpu.VMEM)
    return pl.pallas_call(
        functools.partial(route_kernel, most_rows),
        out_shape=(
            jax.ShapeDtypeStruct((8, rows), jnp.int32),
            jax.ShapeDtypeStruct((devices, 16, columns), jnp.bfloat16),
        ),
        in_specs=[
            pl.BlockSpec(memory_space=pltpu.SMEM),
            vmem,
            pl.BlockSpec(memory_space=pl.ANY),
        ],
        out_specs=(vmem,) * 2,
        compiler_params=pltpu.CompilerParams(vmem_limit_bytes=VMEM_BYTES),
        name="route",
    )(block_counts, dest_slots, after)


def put_rows(slots, rows_ref, owned):
    slot = lax.broadcasted_iota(jnp.int32, (owned, slots.shape[1]), 0)
    put = jnp.where(slot == slots, 1.0, 0.0).astype(jnp.bfloat16)
    return jnp.dot(put, rows_ref[: slots.shape[1], :], preferred_element_type=jnp.float32)


def place_kernel(came_ref, values_ref, slots_ref, started_ref, out_ref):
    devices, tall, columns = came_ref.shape
    most_rows = tall - 16
    owned = out_ref.shape[0]
    total = jnp.zeros(out_ref.shape, jnp.float32)
    me = group_index()
    for other in range(devices):
        source = lax.bitwise_xor(me, other)
        marks = came_ref[source, most_rows:, :].astype(jnp.float32)[0:8].astype(jnp.int32)
        slots_ref[other] = marks[:, :128]
        total += put_rows(marks[0:1, :most_rows], came_ref.at[source], owned)
        if other == 0:
            started_ref[...] = put_rows(marks[0:1, :most_rows], values_ref, owned)
    out_ref[...] = total.astype(jnp.bfloat16)


def place_keys(came, own_values):
    devices, tall, columns = came.shape
    vmem = pl.BlockSpec(memory_space=pltpu.VMEM)
    return pl.pallas_call(
        place_kernel,
        out_shape=(
            jax.ShapeDtypeStruct((devices, 8, 128), jnp.int32),
            jax.ShapeDtypeStruct((OWN_DEV, columns), jnp.float32),
            jax.ShapeDtypeStruct((OWN_DEV, columns), jnp.bfloat16),
        ),
        in_specs=[vmem] * 2,
        out_specs=(vmem,) * 3,
        compiler_params=pltpu.CompilerParams(vmem_limit_bytes=VMEM_PLACE),
        name="place_keys",
    )(came, own_values)


def place_values_kernel(slots_ref, started_ref, *refs):
    out_ref = refs[-1]
    total = started_ref[...]
    for other, rows_ref in enumerate(refs[:-1]):
        slots = slots_ref[other + 1, 0:1, : rows_ref.shape[0]]
        total += put_rows(slots, rows_ref, out_ref.shape[0])
    out_ref[...] = total.astype(jnp.bfloat16)


def place_values(slots, started, came):
    vmem = pl.BlockSpec(memory_space=pltpu.VMEM)
    return pl.pallas_call(
        place_values_kernel,
        out_shape=jax.ShapeDtypeStruct(started.shape, jnp.bfloat16),
        in_specs=[vmem] * (2 + len(came)),
        out_specs=vmem,
        compiler_params=pltpu.CompilerParams(vmem_limit_bytes=VMEM_PLACE),
        name="place_values",
    )(slots, started, *came)


def local(
    tokens,
    norm_gain,
    key_weight,
    value_weight,
    key_bias,
    value_bias,
    block_counts,
    positions,
    dest_slots,
):
    axes = ("rep", "fsdp")
    devices = lax.axis_size(axes)
    most_rows = (HOT_BLOCKS + 1) * (BLOCK // devices)
    capacity = devices * most_rows
    rows, width = tokens.shape
    depth = key_weight.shape[0]
    shards = lax.axis_size("fsdp")

    def exchange(rows_by_owner):
        return lax.all_to_all(rows_by_owner, axes, split_axis=0, concat_axis=0, tiled=True)

    got = lax.ppermute(tokens, "tp", [(0, 1), (1, 0)])
    quarter = depth // 4
    relayed = (
        shards == 2
        and lax.axis_size("groups") == 2
        and lax.axis_size("rep") % 2 == 0
        and depth % 4 == 0
        and quarter % 128 == 0
    )
    swap = [(0, 1), (1, 0)]
    if relayed:
        (key_own,) = cut_quarters((key_weight,), (False,))
        value_own, key_last, value_last = cut_quarters(
            (value_weight, key_weight, value_weight), (False, True, True)
        )
        key_own = lax.ppermute(key_own, "fsdp", swap)
        value_own = lax.ppermute(value_own, "fsdp", swap)
        got, key_last, value_last = ordered(got, key_last, value_last)
        key_last = lax.ppermute(key_last, "fsdp", swap)
        value_last = lax.ppermute(value_last, "fsdp", swap)

    near_keys, near_values, scale = near_part(
        tokens,
        got,
        norm_gain,
        key_weight,
        value_weight,
        key_bias,
        value_bias,
    )
    if relayed:
        across = [(i, i ^ 1) for i in range(lax.axis_size("rep"))]
        key_own, near_values = ordered(key_own, near_values)

        def pieces_of(own, opposite):
            by_group = lax.ppermute(own, "groups", swap)
            by_rep = lax.ppermute(own, "rep", across)
            return own, by_group, by_rep, opposite

        key_pieces = pieces_of(key_own, key_last)
        value_pieces = pieces_of(value_own, value_last)
    else:
        steps = range(1, shards)

        def pieces_of(weight):
            return tuple(
                lax.ppermute(weight, "fsdp", [(i, (i + k) % shards) for i in range(shards)])
                for k in steps
            )

        key_pieces = pieces_of(key_weight)
        value_pieces = pieces_of(value_weight)

    columns = key_weight.shape[1]
    inline = most_rows % 16 == 0 and most_rows <= columns
    target, marks = route(block_counts, dest_slots, devices, most_rows, columns, near_values)
    positions, near_values = ordered(positions, near_values)
    angles = rotary_angles(positions)
    if not inline:
        got_marks = exchange(marks[:, 0, :most_rows].reshape(capacity))
    (send_keys,) = far_part(
        relayed,
        (tokens, got),
        norm_gain,
        near_keys,
        scale,
        key_pieces,
        angles,
        target,
        capacity,
        marks if inline else None,
        1,
        value_pieces[0],
    )
    came_keys = exchange(send_keys)
    paired = inline and devices & (devices - 1) == 0 and most_rows <= 128
    send_values = far_part(
        relayed,
        (tokens, got),
        norm_gain,
        near_values,
        scale,
        value_pieces,
        (),
        target,
        capacity,
        None,
        devices if paired else 1,
        send_keys,
    )
    if paired:
        came_values = list(send_values)
        for other in sorted(range(1, devices), key=lambda k: -(k ^ 2)):
            came_values[other] = lax.ppermute(
                send_values[other], axes, [(i, i ^ other) for i in range(devices)]
            )
        slots, started, cache_keys = place_keys(came_keys, send_values[0])
        return cache_keys, place_values(slots, started, came_values[1:])
    came_values = exchange(send_values[0])
    if inline:
        got_marks = came_keys[:, most_rows, :most_rows].reshape(capacity)
        came_keys = came_keys[:, :most_rows].reshape(capacity, columns)
    put = (
        jnp.arange(OWN_DEV, dtype=jnp.int32)[:, None] == got_marks.astype(jnp.int32)[None, :]
    ).astype(jnp.bfloat16)
    return tuple(
        jnp.dot(put, came, preferred_element_type=jnp.float32).astype(jnp.bfloat16)
        for came in (came_keys, came_values)
    )


def solution(mesh):
    return jax.shard_map(
        local,
        mesh=mesh,
        in_specs=(
            P(("groups", "rep", "fsdp"), "tp"),
            P(),
            P("fsdp", "tp"),
            P("fsdp", "tp"),
            P("tp"),
            P("tp"),
            P("groups"),
            P(("groups", "rep", "fsdp")),
            P(("groups", "rep", "fsdp")),
        ),
        out_specs=(P(("groups", "rep", "fsdp"), "tp"), P(("groups", "rep", "fsdp"), "tp")),
        check_vma=False,
    )
```
